32 devices in a mesh: mem: 4 (over z), lon: 8 (over y, x, core).
Axes of the slice: x: 2, y: 2, z: 4, core: 2. Of those that a mesh axis runs over, the one named last changes fastest.
Arguments:
- fields: bfloat16 [20, 64, 64, 128], P('mem', None, 'lon'), may hold values from -8 to 8
- w_query: bfloat16 [24, 576], replicated, may hold values from -1 to 1
- w_key: bfloat16 [24, 576], replicated, may hold values from -1 to 1
- w_value: bfloat16 [24, 576], replicated, may hold values from -0.25 to 0.25
- w_out: bfloat16 [64, 216], replicated, may hold values from -1.25 to 1.25
Outputs:
- updated: bfloat16 [20, 64, 64, 128], P('mem', None, 'lon')
The draws below stay inside these ranges and needn't reach their ends.
All inputs are finite; a program needn't handle non-finite values.
Results may differ from the reference program's by a relative error of at most 0.008.
Values may be sent and summed in bfloat16 or wider, within the bound.
A program may use at most 64 MiB of HBM per device.

```python
import math
import jax
import jax.numpy as jnp
from jax import lax

CH = 64
CQ = 24
LAT = 128
MEMBERS = 20
LON = 64


def draw_fields(key, part):
    full_shape = (MEMBERS, CH, LON, LAT)
    shared_shape = (1, CH, LON, LAT)
    ramp = 0.45 + 0.9 * jnp.arange(LON, dtype=jnp.float32) / max(LON - 1, 1)
    ramp = ramp.reshape(1, 1, LON, 1)
    shared = jax.random.normal(jax.random.fold_in(key, 7), shared_shape, jnp.float32)
    own = jax.random.normal(jax.random.fold_in(key, 8), full_shape, jnp.float32)
    sample = ramp * (0.6 * shared + 0.8 * own)
    return jnp.clip(sample, -8.0, 8.0).astype(jnp.bfloat16)


def query_weight(key):
    fan_in = 9 * CH
    first_draw = jax.random.normal(jax.random.fold_in(key, 21), (CQ, 9 * CH), jnp.float32) / math.sqrt(fan_in)
    return jnp.clip(first_draw, -1.0, 1.0)


def draw_w_query(key, part):
    return query_weight(key).astype(jnp.bfloat16)


def draw_w_key(key, part):
    half = CH // 2
    rounded = query_weight(key).astype(jnp.bfloat16).astype(jnp.float32)
    shaped = rounded.reshape(CQ, 9, CH)
    factor = jnp.exp(jax.random.uniform(jax.random.fold_in(key, 23), (CQ, 9, half), jnp.float32, math.log(0.5), math.log(2.0)))
    key_weight = jnp.concatenate([factor * shaped[:, :, half:], -factor * shaped[:, :, :half]], axis=2)
    return jnp.clip(key_weight.reshape(CQ, 9 * CH), -1.0, 1.0).astype(jnp.bfloat16)


def bell_draw(stream_key, dims, width, bound, kind=jnp.bfloat16):
    return jnp.clip(width * jax.random.normal(stream_key, dims, jnp.float32), -bound, bound).astype(kind)


def setup_inputs(seed: int = 0) -> dict:
    key_of = jax.random.split(jax.random.key(seed), 6)
    fields = draw_fields(jax.random.fold_in(key_of[5], 71), 0)
    w_query = draw_w_query(jax.random.fold_in(key_of[5], 71), 0)
    w_key = draw_w_key(jax.random.fold_in(key_of[5], 71), 0)
    w_value = bell_draw(key_of[3], (CQ, 9 * CH), (9 * CH) ** -0.5, 0.25)
    w_out = bell_draw(key_of[4], (CH, 9 * CQ), CQ ** -0.5, 1.25)
    return dict(fields=fields, w_query=w_query, w_key=w_key, w_value=w_value, w_out=w_out)


def conv_member(member_field, weight):
    channels, longitudes, latitudes = member_field.shape
    wrapped = jnp.concatenate([member_field[:, -1:], member_field, member_field[:, :1]], axis=1)
    padded = jnp.pad(wrapped, ((0, 0), (0, 0), (1, 1)))
    patches = jnp.concatenate([padded[:, lon_step:lon_step + longitudes, lat_step:lat_step + latitudes] for lon_step in range(3) for lat_step in range(3)], axis=0)
    result = jnp.dot(weight, patches.reshape(9 * channels, longitudes * latitudes), preferred_element_type=jnp.float32)
    return result.reshape(weight.shape[0], longitudes, latitudes)

def reference(fields, w_query, w_key, w_value, w_out):
    w_inner = jnp.concatenate([w_query, w_key, w_value], axis=0)

    def project(member_field):
        return conv_member(member_field, w_inner).astype(jnp.bfloat16)
    projected = lax.map(project, fields)
    queries = projected[:, :CQ].reshape(MEMBERS, -1)
    keys_all = projected[:, CQ:2 * CQ].reshape(MEMBERS, -1)
    values = projected[:, 2 * CQ:]
    gram_sums = jnp.dot(queries, keys_all.T, preferred_element_type=jnp.float32)
    score_scale = 1.0 / math.sqrt(CQ * LAT * LON)
    weights = jax.nn.softmax(gram_sums * score_scale, axis=1).astype(jnp.bfloat16)
    mixed_values = jnp.dot(weights, values.reshape(MEMBERS, -1), preferred_element_type=jnp.float32)
    mixed_values = mixed_values.astype(jnp.bfloat16).reshape(values.shape)

    def finish(member_pair):
        member_field, member_mixed = member_pair
        return (member_field.astype(jnp.float32) + conv_member(member_mixed, w_out)).astype(jnp.bfloat16)
    return lax.map(finish, (fields, mixed_values))
```

```python
import functools
import math

import jax
import jax.numpy as jnp
from jax import lax
from jax.experimental import pallas as pl
from jax.experimental.pallas import tpu as pltpu
from jax.sharding import PartitionSpec as P

MESH = pl.DeviceIdType.MESH
F32 = jnp.float32
BF16 = jnp.bfloat16


def with_halo(block, sides, width):
    for axis, dim in sides:
        count = lax.axis_size(axis)
        forward = [(i, i + 1) for i in range(count - 1)]
        forward.append((count - 1, 0))
        backward = [(target, source) for source, target in forward]
        low = lax.ppermute(
            lax.slice_in_dim(block, block.shape[dim] - width, None, axis=dim), axis, forward
        )
        high = lax.ppermute(lax.slice_in_dim(block, 0, width, axis=dim), axis, backward)
        block = jnp.concatenate([low, block, high], axis=dim)
    return block


def tap_stack(extended):
    span_lon = extended.shape[2] - 2
    latitudes = extended.shape[3]
    padded = jnp.pad(extended, ((0, 0), (0, 0), (0, 0), (1, 1)))
    return jnp.concatenate(
        [
            padded[:, :, lon_step : lon_step + span_lon, lat_step : lat_step + latitudes]
            for lon_step in range(3)
            for lat_step in range(3)
        ],
        axis=1,
    )


def plain_shards(fields, w_query, w_key, w_value, w_out):
    members = fields.shape[0]
    longitudes = fields.shape[2]
    latitudes = fields.shape[3]
    inner_width = w_query.shape[0]
    extended = with_halo(fields, (("lon", 2),), 1)
    w_inner = jnp.concatenate([w_query, w_key, w_value], axis=0)
    projected = jnp.einsum(
        "oc,mcwh->mowh", w_inner, tap_stack(extended), preferred_element_type=jnp.float32
    ).astype(jnp.bfloat16)
    queries = projected[:, :inner_width]
    keys_local = projected[:, inner_width : 2 * inner_width]
    values = projected[:, 2 * inner_width :]
    query_blocks, key_blocks = (
        lax.all_to_all(queries, "mem", split_axis=3, concat_axis=0, tiled=True),
        lax.all_to_all(keys_local, "mem", split_axis=3, concat_axis=0, tiled=True),
    )
    total_members = query_blocks.shape[0]
    partial_value = jnp.dot(
        query_blocks.reshape(total_members, -1),
        key_blocks.reshape(total_members, -1).T,
        preferred_element_type=jnp.float32,
    )
    score_scale = 1.0 / math.sqrt(inner_width * latitudes * longitudes * lax.axis_size("lon"))
    first_row = lax.axis_index("mem") * members
    gram_sums = lax.psum(partial_value, ("mem", "lon"))
    weights_all = jax.nn.softmax(gram_sums * score_scale, axis=1).astype(jnp.bfloat16)
    weights_own = lax.dynamic_slice_in_dim(weights_all, first_row, members, 0)
    mixed_values = jnp.einsum(
        "mn,ncwh->mcwh",
        weights_own,
        lax.all_gather(values, "mem", axis=0, tiled=True),
        preferred_element_type=jnp.float32,
    ).astype(jnp.bfloat16)
    mixed_ext = with_halo(mixed_values, (("lon", 2),), 1)
    branch = jnp.einsum(
        "oc,mcwh->mowh", w_out, tap_stack(mixed_ext), preferred_element_type=jnp.float32
    )
    return (fields.astype(jnp.float32) + branch).astype(jnp.bfloat16)


def lat_taps(block, lat):
    width = block.shape[1]
    lane = lax.broadcasted_iota(jnp.int32, block.shape, 1) & (lat - 1)
    low = jnp.where(lane == 0, 0.0, pltpu.roll(block, 1, 1))
    high = jnp.where(lane == lat - 1, 0.0, pltpu.roll(block, width - 1, 1))
    return jnp.concatenate([low, block, high], axis=0).astype(BF16)


def layer_kernel(
    dims, f_ref, wi_ref, wo_ref, out_ref,
    y_ref, halo, qk_out, qk_all, v_all, g_out, g_mem, g_lon, mixed, edge_out, edge_in,
    halo_s, halo_r, qk_s, qk_r, v_s, v_r, gm_s, gm_r, gl_s, gl_r, edge_s, edge_r,
):
    mems, lons, members, ch, cq, cols, lat, score_scale = dims
    wide = cols * lat
    half = wide // 2
    piece = wide // mems
    total = mems * members
    z = lax.axis_index("mem")
    s = lax.axis_index("lon")
    right = lax.rem(s + 1, lons)
    left = lax.rem(s + lons - 1, lons)

    def mem_peer(d):
        return lax.rem(z + d, mems)

    def lon_peer(d):
        return lax.rem(s + d, lons)

    barrier = pltpu.get_barrier_semaphore()
    for d in range(1, mems):
        pl.semaphore_signal(barrier, inc=1, device_id={"mem": mem_peer(d)}, device_id_type=MESH)
    for d in range(1, lons):
        pl.semaphore_signal(barrier, inc=1, device_id={"lon": lon_peer(d)}, device_id_type=MESH)
    pl.semaphore_wait(barrier, mems + lons - 2)

    def remote(src, dst, send, recv, device):
        return pltpu.make_async_remote_copy(
            src_ref=src, dst_ref=dst, send_sem=send, recv_sem=recv, device_id=device, device_id_type=MESH
        )

    halo_copies = [
        remote(f_ref.at[:, :, pl.ds(wide - lat, lat)], halo.at[0], halo_s.at[0], halo_r.at[0], {"lon": right}),
        remote(f_ref.at[:, :, pl.ds(0, lat)], halo.at[1], halo_s.at[1], halo_r.at[1], {"lon": left}),
    ]
    for copy in halo_copies:
        copy.start()

    inner = 3 * cq
    for m in range(members):
        taps = lat_taps(f_ref[m].astype(F32), lat)
        y_ref[m] = jnp.dot(wi_ref[...], taps, preferred_element_type=F32)
    for copy in halo_copies:
        copy.wait_recv()
    qk_copies = []
    for d in range(1, mems):
        qk_copies.append(
            remote(qk_out.at[mem_peer(d)], qk_all.at[z], qk_s.at[d - 1], qk_r.at[d - 1], {"mem": mem_peer(d)})
        )
    for m in range(members):
        from_left = jnp.dot(wi_ref[0:inner], lat_taps(halo[0, m].astype(F32), lat), preferred_element_type=F32)
        from_right = jnp.dot(wi_ref[2 * inner :], lat_taps(halo[1, m].astype(F32), lat), preferred_element_type=F32)
        projected = (
            y_ref[m, inner : 2 * inner]
            + jnp.concatenate([from_left, y_ref[m, 0:inner, 0 : wide - lat]], axis=1)
            + jnp.concatenate([y_ref[m, 2 * inner :, lat:], from_right], axis=1)
        )
        queries_keys = projected[0 : 2 * cq].astype(BF16)
        for p in range(mems):
            qk_out[p, m] = queries_keys[:, p * piece : (p + 1) * piece]
        values = projected[2 * cq :]
        v_all[z, m] = jnp.concatenate([values[:, :half], values[:, half:]], axis=0).astype(BF16)
        for d in range(1, mems):
            remote(
                qk_out.at[mem_peer(d), m], qk_all.at[z, m], qk_s.at[d - 1], qk_r.at[d - 1], {"mem": mem_peer(d)}
            ).start()
    v_copies = [
        remote(v_all.at[z], v_all.at[z], v_s.at[d - 1], v_r.at[d - 1], {"mem": mem_peer(d)})
        for d in range(1, mems)
    ]
    for copy in v_copies:
        copy.start()

    qk_all[z] = qk_out[z]
    column = lax.broadcasted_iota(jnp.int32, (cq, total * cq), 1).astype(F32)
    row = lax.broadcasted_iota(jnp.int32, (cq, total * cq), 0).astype(F32)
    same = jnp.where(column - cq * jnp.floor((column + 0.5) / cq) == row, 1.0, 0.0)
    spread = lax.broadcasted_iota(jnp.int32, (total * cq, 128), 0) - cq * lax.broadcasted_iota(
        jnp.int32, (total * cq, 128), 1
    )
    groups = jnp.where((spread >= 0) & (spread < cq), 1.0, 0.0)
    for copy in qk_copies:
        copy.wait_recv()
    both = qk_all[...].astype(F32).reshape(total, 2 * cq, piece)
    queries = both[:, :cq].reshape(total * cq, piece).astype(BF16)
    keys = both[:, cq:].reshape(total * cq, piece).astype(BF16)
    products = lax.dot_general(queries, keys, (((1,), (1,)), ((), ())), preferred_element_type=F32)
    by_member = jnp.sum(products.reshape(total, cq, total * cq) * same[None], axis=1)
    gram = jnp.dot(by_member, groups, precision=lax.Precision.HIGHEST, preferred_element_type=F32)
    filler = jnp.zeros((8 - members, 128), F32)
    for p in range(mems):
        g_out[p] = jnp.concatenate([gram[p * members : (p + 1) * members], filler], axis=0)
    gm_copies = [
        remote(g_out.at[mem_peer(d)], g_mem.at[z], gm_s.at[d - 1], gm_r.at[d - 1], {"mem": mem_peer(d)})
        for d in range(1, mems)
    ]
    for copy in gm_copies:
        copy.start()
    g_mem[z] = g_out[z]
    for copy in gm_copies:
        copy.wait_recv()
    g_lon[s] = jnp.sum(g_mem[...], axis=0)
    gl_copies = [
        remote(g_lon.at[s], g_lon.at[s], gl_s.at[d - 1], gl_r.at[d - 1], {"lon": lon_peer(d)})
        for d in range(1, lons)
    ]
    for copy in gl_copies:
        copy.start()
    for copy in gl_copies:
        copy.wait_recv()
    lane = lax.broadcasted_iota(jnp.int32, (8, 128), 1)
    scores = jnp.where(lane < total, jnp.sum(g_lon[...], axis=0) * score_scale, -jnp.inf)
    powers = jnp.exp(scores - jnp.max(scores, axis=1, keepdims=True))
    weights = (powers / jnp.sum(powers, axis=1, keepdims=True)).astype(BF16).astype(F32)

    for copy in v_copies:
        copy.wait_recv()
    steps = cols // 2
    edge_copies = [
        remote(edge_out.at[0], edge_in.at[0], edge_s.at[0], edge_r.at[0], {"lon": right}),
        remote(edge_out.at[1], edge_in.at[1], edge_s.at[1], edge_r.at[1], {"lon": left}),
    ]
    edge_pad = jnp.zeros((edge_out.shape[2] - cq, lat), F32)
    for t in [0, steps - 1] + list(range(1, steps - 1)):
        sums = [None] * members
        for n in range(total):
            block = v_all[n // members, n % members, :, t * lat : (t + 1) * lat].astype(F32)
            for m in range(members):
                term = weights[m : m + 1, n : n + 1] * block
                sums[m] = term if n == 0 else sums[m] + term
        for m in range(members):
            rounded = sums[m].astype(BF16).astype(F32)
            mixed[m, :, t * lat : (t + 1) * lat] = rounded[:cq]
            mixed[m, :, half + t * lat : half + (t + 1) * lat] = rounded[cq:]
            if t == 0:
                edge_out[1, m] = jnp.concatenate([rounded[:cq], edge_pad], axis=0).astype(BF16)
            if t == steps - 1:
                edge_out[0, m] = jnp.concatenate([rounded[cq:], edge_pad], axis=0).astype(BF16)
        if t == 0:
            edge_copies[1].start()
        if t == steps - 1:
            edge_copies[0].start()
    for m in range(members):
        y_ref[m, 0 : 3 * ch] = jnp.dot(wo_ref[...], lat_taps(mixed[m], lat), preferred_element_type=F32)
    for copy in edge_copies:
        copy.wait_recv()
    for m in range(members):
        from_left = jnp.dot(wo_ref[0:ch], lat_taps(edge_in[0, m].astype(F32)[:cq], lat), preferred_element_type=F32)
        from_right = jnp.dot(wo_ref[2 * ch :], lat_taps(edge_in[1, m].astype(F32)[:cq], lat), preferred_element_type=F32)
        branch = (
            y_ref[m, ch : 2 * ch]
            + jnp.concatenate([from_left, y_ref[m, 0:ch, 0 : wide - lat]], axis=1)
            + jnp.concatenate([y_ref[m, 2 * ch : 3 * ch, lat:], from_right], axis=1)
        )
        out_ref[m] = (f_ref[m].astype(F32) + branch).astype(BF16)
    for copy in halo_copies + qk_copies + v_copies + gm_copies + gl_copies + edge_copies:
        copy.wait_send()


def shards(mems, lons, fields, w_query, w_key, w_value, w_out):
    members, ch, cols, lat = fields.shape
    cq = w_query.shape[0]
    wide = cols * lat
    if cols % mems or cols % 2 or lat != 128 or members > 8 or (2 * cq) % 16 or ch % 16:
        return plain_shards(fields, w_query, w_key, w_value, w_out)
    w_inner = jnp.concatenate([w_query, w_key, w_value], axis=0)
    w_inner = w_inner.reshape(3 * cq, 3, 3 * ch).transpose(1, 0, 2).reshape(9 * cq, 3 * ch)
    w_outer = w_out.reshape(ch, 3, 3 * cq).transpose(1, 0, 2).reshape(3 * ch, 3 * cq)
    score_scale = 1.0 / math.sqrt(cq * lat * cols * lons)
    dims = (mems, lons, members, ch, cq, cols, lat, score_scale)
    edge_rows = -(-cq // 16) * 16
    dma = pltpu.SemaphoreType.DMA
    vmem = pl.BlockSpec(memory_space=pltpu.VMEM)
    updated = pl.pallas_call(
        functools.partial(layer_kernel, dims),
        out_shape=jax.ShapeDtypeStruct((members, ch, wide), BF16),
        in_specs=[vmem] * 3,
        out_specs=vmem,
        scratch_shapes=[
            pltpu.VMEM((members, max(9 * cq, 3 * ch), wide), F32),
            pltpu.VMEM((2, members, ch, lat), BF16),
            pltpu.VMEM((mems, members, 2 * cq, wide // mems), BF16),
            pltpu.VMEM((mems, members, 2 * cq, wide // mems), BF16),
            pltpu.VMEM((mems, members, 2 * cq, wide // 2), BF16),
            pltpu.VMEM((mems, 8, 128), F32),
            pltpu.VMEM((mems, 8, 128), F32),
            pltpu.VMEM((lons, 8, 128), F32),
            pltpu.VMEM((members, cq, wide), F32),
            pltpu.VMEM((2, members, edge_rows, lat), BF16),
            pltpu.VMEM((2, members, edge_rows, lat), BF16),
            dma((2,)), dma((2,)),
            dma((mems - 1,)), dma((mems - 1,)),
            dma((mems - 1,)), dma((mems - 1,)),
            dma((mems - 1,)), dma((mems - 1,)),
            dma((lons - 1,)), dma((lons - 1,)),
            dma((2,)), dma((2,)),
        ],
        compiler_params=pltpu.CompilerParams(
            collective_id=0, has_side_effects=True, vmem_limit_bytes=40 * 1024 * 1024
        ),
    )(fields.reshape(members, ch, wide), w_inner, w_outer)
    return updated.reshape(members, ch, cols, lat)


def solution(mesh):
    return jax.shard_map(
        functools.partial(shards, mesh.shape["mem"], mesh.shape["lon"]),
        mesh=mesh,
        in_specs=(P("mem", None, "lon", None), P(), P(), P(), P()),
        out_specs=P("mem", None, "lon", None),
        check_vma=False,
    )
```

```python
import functools
import math

import jax
import jax.numpy as jnp
from jax import lax
from jax.experimental import pallas as pl
from jax.experimental.pallas import tpu as pltpu
from jax.sharding import PartitionSpec as P

MESH = pl.DeviceIdType.MESH
F32 = jnp.float32
BF16 = jnp.bfloat16


def with_halo(block, sides, width):
    for axis, dim in sides:
        count = lax.axis_size(axis)
        forward = [(i, i + 1) for i in range(count - 1)]
        forward.append((count - 1, 0))
        backward = [(target, source) for source, target in forward]
        low = lax.ppermute(
            lax.slice_in_dim(block, block.shape[dim] - width, None, axis=dim), axis, forward
        )
        high = lax.ppermute(lax.slice_in_dim(block, 0, width, axis=dim), axis, backward)
        block = jnp.concatenate([low, block, high], axis=dim)
    return block


def tap_stack(extended):
    span_lon = extended.shape[2] - 2
    latitudes = extended.shape[3]
    padded = jnp.pad(extended, ((0, 0), (0, 0), (0, 0), (1, 1)))
    return jnp.concatenate(
        [
            padded[:, :, lon_step : lon_step + span_lon, lat_step : lat_step + latitudes]
            for lon_step in range(3)
            for lat_step in range(3)
        ],
        axis=1,
    )


def plain_shards(fields, w_query, w_key, w_value, w_out):
    members = fields.shape[0]
    longitudes = fields.shape[2]
    latitudes = fields.shape[3]
    inner_width = w_query.shape[0]
    extended = with_halo(fields, (("lon", 2),), 1)
    w_inner = jnp.concatenate([w_query, w_key, w_value], axis=0)
    projected = jnp.einsum(
        "oc,mcwh->mowh", w_inner, tap_stack(extended), preferred_element_type=jnp.float32
    ).astype(jnp.bfloat16)
    queries = projected[:, :inner_width]
    keys_local = projected[:, inner_width : 2 * inner_width]
    values = projected[:, 2 * inner_width :]
    query_blocks, key_blocks = (
        lax.all_to_all(queries, "mem", split_axis=3, concat_axis=0, tiled=True),
        lax.all_to_all(keys_local, "mem", split_axis=3, concat_axis=0, tiled=True),
    )
    total_members = query_blocks.shape[0]
    partial_value = jnp.dot(
        query_blocks.reshape(total_members, -1),
        key_blocks.reshape(total_members, -1).T,
        preferred_element_type=jnp.float32,
    )
    score_scale = 1.0 / math.sqrt(inner_width * latitudes * longitudes * lax.axis_size("lon"))
    first_row = lax.axis_index("mem") * members
    gram_sums = lax.psum(partial_value, ("mem", "lon"))
    weights_all = jax.nn.softmax(gram_sums * score_scale, axis=1).astype(jnp.bfloat16)
    weights_own = lax.dynamic_slice_in_dim(weights_all, first_row, members, 0)
    mixed_values = jnp.einsum(
        "mn,ncwh->mcwh",
        weights_own,
        lax.all_gather(values, "mem", axis=0, tiled=True),
        preferred_element_type=jnp.float32,
    ).astype(jnp.bfloat16)
    mixed_ext = with_halo(mixed_values, (("lon", 2),), 1)
    branch = jnp.einsum(
        "oc,mcwh->mowh", w_out, tap_stack(mixed_ext), preferred_element_type=jnp.float32
    )
    return (fields.astype(jnp.float32) + branch).astype(jnp.bfloat16)


def lat_taps(block, lat):
    width = block.shape[1]
    lane = lax.broadcasted_iota(jnp.int32, block.shape, 1) & (lat - 1)
    low = jnp.where(lane == 0, 0.0, pltpu.roll(block, 1, 1))
    high = jnp.where(lane == lat - 1, 0.0, pltpu.roll(block, width - 1, 1))
    return jnp.concatenate([low, block, high], axis=0).astype(BF16)


def layer_kernel(
    dims, f_ref, wq_ref, wk_ref, wv_ref, w_out_ref, out_ref,
    wi_ref, wo_ref, y_ref, halo, qk_out, qk_all, v_all, g_out, g_mem, g_lon, acc, mixed, edge_out, edge_in,
    halo_s, halo_r, qk_s, qk_r, v_s, v_r, gm_s, gm_r, gl_s, gl_r, edge_s, edge_r,
):
    mems, lons, members, ch, cq, cols, lat, score_scale = dims
    wide = cols * lat
    half = wide // 2
    piece = wide // mems
    total = mems * members
    z = lax.axis_index("mem")
    s = lax.axis_index("lon")
    right = lax.rem(s + 1, lons)
    left = lax.rem(s + lons - 1, lons)

    def mem_peer(d):
        return lax.rem(z + d, mems)

    def lon_peer(d):
        return lax.rem(s + d, lons)

    barrier = pltpu.get_barrier_semaphore()
    for d in range(1, mems):
        pl.semaphore_signal(barrier, inc=1, device_id={"mem": mem_peer(d)}, device_id_type=MESH)
    for d in range(1, lons):
        pl.semaphore_signal(barrier, inc=1, device_id={"lon": lon_peer(d)}, device_id_type=MESH)
    w_inner = jnp.concatenate([ref[...].astype(F32) for ref in (wq_ref, wk_ref, wv_ref)], axis=0)
    w_outer = w_out_ref[...].astype(F32)
    wi_ref[...] = jnp.concatenate([w_inner[:, a * 3 * ch : (a + 1) * 3 * ch] for a in range(3)], axis=0).astype(BF16)
    wo_ref[...] = jnp.concatenate([w_outer[:, a * 3 * cq : (a + 1) * 3 * cq] for a in range(3)], axis=0).astype(BF16)
    pl.semaphore_wait(barrier, mems + lons - 2)

    def remote(src, dst, send, recv, device):
        return pltpu.make_async_remote_copy(
            src_ref=src, dst_ref=dst, send_sem=send, recv_sem=recv, device_id=device, device_id_type=MESH
        )

    halo_copies = [
        remote(f_ref.at[:, :, pl.ds(wide - lat, lat)], halo.at[0], halo_s.at[0], halo_r.at[0], {"lon": right}),
        remote(f_ref.at[:, :, pl.ds(0, lat)], halo.at[1], halo_s.at[1], halo_r.at[1], {"lon": left}),
    ]
    for copy in halo_copies:
        copy.start()

    inner = 3 * cq
    for m in range(members):
        taps = lat_taps(f_ref[m].astype(F32), lat)
        y_ref[m] = jnp.dot(wi_ref[...], taps, preferred_element_type=F32)
    for copy in halo_copies:
        copy.wait_recv()
    qk_copies = []
    for d in range(1, mems):
        qk_copies.append(
            remote(qk_out.at[mem_peer(d)], qk_all.at[z], qk_s.at[d - 1], qk_r.at[d - 1], {"mem": mem_peer(d)})
        )
    for m in range(members):
        from_left = jnp.dot(wi_ref[0:inner], lat_taps(halo[0, m].astype(F32), lat), preferred_element_type=F32)
        from_right = jnp.dot(wi_ref[2 * inner :], lat_taps(halo[1, m].astype(F32), lat), preferred_element_type=F32)
        projected = (
            y_ref[m, inner : 2 * inner]
            + jnp.concatenate([from_left, y_ref[m, 0:inner, 0 : wide - lat]], axis=1)
            + jnp.concatenate([y_ref[m, 2 * inner :, lat:], from_right], axis=1)
        )
        queries_keys = projected[0 : 2 * cq].astype(BF16)
        for p in range(mems):
            qk_out[p, m] = queries_keys[:, p * piece : (p + 1) * piece]
        values = projected[2 * cq :]
        v_all[z, m] = jnp.concatenate([values[:, :half], values[:, half:]], axis=0).astype(BF16)
        for d in range(1, mems):
            remote(
                qk_out.at[mem_peer(d), m], qk_all.at[z, m], qk_s.at[d - 1], qk_r.at[d - 1], {"mem": mem_peer(d)}
            ).start()
    v_copies = [
        remote(v_all.at[z], v_all.at[z], v_s.at[d - 1], v_r.at[d - 1], {"mem": mem_peer(d)})
        for d in range(1, mems)
    ]
    for copy in qk_copies:
        copy.wait_send()
    for copy in v_copies:
        copy.start()

    qk_all[z] = qk_out[z]
    column = lax.broadcasted_iota(jnp.int32, (cq, total * cq), 1).astype(F32)
    row = lax.broadcasted_iota(jnp.int32, (cq, total * cq), 0).astype(F32)
    same = jnp.where(column - cq * jnp.floor((column + 0.5) / cq) == row, 1.0, 0.0)
    spread = lax.broadcasted_iota(jnp.int32, (total * cq, 128), 0) - cq * lax.broadcasted_iota(
        jnp.int32, (total * cq, 128), 1
    )
    groups = jnp.where((spread >= 0) & (spread < cq), 1.0, 0.0)
    for copy in qk_copies:
        copy.wait_recv()
    both = qk_all[...].astype(F32).reshape(total, 2 * cq, piece)
    queries = both[:, :cq].reshape(total * cq, piece).astype(BF16)
    keys = both[:, cq:].reshape(total * cq, piece).astype(BF16)
    products = lax.dot_general(queries, keys, (((1,), (1,)), ((), ())), preferred_element_type=F32)
    by_member = jnp.sum(products.reshape(total, cq, total * cq) * same[None], axis=1)
    gram = jnp.dot(by_member, groups, precision=lax.Precision.HIGHEST, preferred_element_type=F32)
    filler = jnp.zeros((8 - members, 128), F32)
    for p in range(mems):
        g_out[p] = jnp.concatenate([gram[p * members : (p + 1) * members], filler], axis=0)
    gm_copies = [
        remote(g_out.at[mem_peer(d)], g_mem.at[z], gm_s.at[d - 1], gm_r.at[d - 1], {"mem": mem_peer(d)})
        for d in range(1, mems)
    ]
    for copy in gm_copies:
        copy.start()
    g_mem[z] = g_out[z]
    for copy in gm_copies:
        copy.wait_recv()
    g_lon[s] = jnp.sum(g_mem[...], axis=0)
    gl_copies = [
        remote(g_lon.at[s], g_lon.at[s], gl_s.at[d - 1], gl_r.at[d - 1], {"lon": lon_peer(d)})
        for d in range(1, lons)
    ]
    for copy in gl_copies:
        copy.start()
    for copy in gl_copies:
        copy.wait_recv()
    lane = lax.broadcasted_iota(jnp.int32, (8, 128), 1)
    scores = jnp.where(lane < total, jnp.sum(g_lon[...], axis=0) * score_scale, -jnp.inf)
    powers = jnp.exp(scores - jnp.max(scores, axis=1, keepdims=True))
    weights = (powers / jnp.sum(powers, axis=1, keepdims=True)).astype(BF16).astype(F32)

    steps = cols // 2
    edge_copies = [
        remote(edge_out.at[0], edge_in.at[0], edge_s.at[0], edge_r.at[0], {"lon": right}),
        remote(edge_out.at[1], edge_in.at[1], edge_s.at[1], edge_r.at[1], {"lon": left}),
    ]
    edge_pad = jnp.zeros((edge_out.shape[2] - cq, lat), F32)
    for d in range(mems):
        source = lax.rem(z + mems - d, mems)
        share = weights[:, 0:members]
        for p in range(1, mems):
            share = jnp.where(source == p, weights[:, p * members : (p + 1) * members], share)
        if d > 0:
            v_copies[d - 1].wait_recv()
        for t in [0, steps - 1] + list(range(1, steps - 1)):
            lanes = slice(t * lat, (t + 1) * lat)
            sums = [None if d == 0 else acc[m, :, lanes] for m in range(members)]
            for n in range(members):
                block = v_all[source, n, :, lanes].astype(F32)
                for m in range(members):
                    term = share[m : m + 1, n : n + 1] * block
                    sums[m] = term if sums[m] is None else sums[m] + term
            for m in range(members):
                if d < mems - 1:
                    acc[m, :, lanes] = sums[m]
                    continue
                rounded = sums[m].astype(BF16).astype(F32)
                mixed[m, :, t * lat : (t + 1) * lat] = rounded[:cq]
                mixed[m, :, half + t * lat : half + (t + 1) * lat] = rounded[cq:]
                if t == 0:
                    edge_out[1, m] = jnp.concatenate([rounded[:cq], edge_pad], axis=0).astype(BF16)
                if t == steps - 1:
                    edge_out[0, m] = jnp.concatenate([rounded[cq:], edge_pad], axis=0).astype(BF16)
            if d == mems - 1 and t == 0:
                edge_copies[1].start()
            if d == mems - 1 and t == steps - 1:
                edge_copies[0].start()
    for m in range(members):
        y_ref[m, 0 : 3 * ch] = jnp.dot(wo_ref[...], lat_taps(mixed[m], lat), preferred_element_type=F32)
    for copy in edge_copies:
        copy.wait_recv()
    for m in range(members):
        from_left = jnp.dot(wo_ref[0:ch], lat_taps(edge_in[0, m].astype(F32)[:cq], lat), preferred_element_type=F32)
        from_right = jnp.dot(wo_ref[2 * ch :], lat_taps(edge_in[1, m].astype(F32)[:cq], lat), preferred_element_type=F32)
        branch = (
            y_ref[m, ch : 2 * ch]
            + jnp.concatenate([from_left, y_ref[m, 0:ch, 0 : wide - lat]], axis=1)
            + jnp.concatenate([y_ref[m, 2 * ch : 3 * ch, lat:], from_right], axis=1)
        )
        out_ref[m] = (f_ref[m].astype(F32) + branch).astype(BF16)
    for copy in halo_copies + v_copies + gm_copies + gl_copies + edge_copies:
        copy.wait_send()


def shards(mems, lons, fields, w_query, w_key, w_value, w_out):
    members, ch, cols, lat = fields.shape
    cq = w_query.shape[0]
    wide = cols * lat
    if cols % mems or cols % 2 or lat != 128 or members > 8 or (2 * cq) % 16 or ch % 16:
        return plain_shards(fields, w_query, w_key, w_value, w_out)
    score_scale = 1.0 / math.sqrt(cq * lat * cols * lons)
    dims = (mems, lons, members, ch, cq, cols, lat, score_scale)
    edge_rows = -(-cq // 16) * 16
    dma = pltpu.SemaphoreType.DMA
    vmem = pl.BlockSpec(memory_space=pltpu.VMEM)
    updated = pl.pallas_call(
        functools.partial(layer_kernel, dims),
        out_shape=jax.ShapeDtypeStruct((members, ch, wide), BF16),
        in_specs=[vmem] * 5,
        out_specs=vmem,
        scratch_shapes=[
            pltpu.VMEM((9 * cq, 3 * ch), BF16),
            pltpu.VMEM((3 * ch, 3 * cq), BF16),
            pltpu.VMEM((members, max(9 * cq, 3 * ch), wide), F32),
            pltpu.VMEM((2, members, ch, lat), BF16),
            pltpu.VMEM((mems, members, 2 * cq, wide // mems), BF16),
            pltpu.VMEM((mems, members, 2 * cq, wide // mems), BF16),
            pltpu.VMEM((mems, members, 2 * cq, wide // 2), BF16),
            pltpu.VMEM((mems, 8, 128), F32),
            pltpu.VMEM((mems, 8, 128), F32),
            pltpu.VMEM((lons, 8, 128), F32),
            pltpu.VMEM((members, 2 * cq, wide // 2), F32),
            pltpu.VMEM((members, cq, wide), F32),
            pltpu.VMEM((2, members, edge_rows, lat), BF16),
            pltpu.VMEM((2, members, edge_rows, lat), BF16),
            dma((2,)), dma((2,)),
            dma((mems - 1,)), dma((mems - 1,)),
            dma((mems - 1,)), dma((mems - 1,)),
            dma((mems - 1,)), dma((mems - 1,)),
            dma((lons - 1,)), dma((lons - 1,)),
            dma((2,)), dma((2,)),
        ],
        compiler_params=pltpu.CompilerParams(
            collective_id=0, has_side_effects=True, vmem_limit_bytes=40 * 1024 * 1024
        ),
    )(fields.reshape(members, ch, wide), w_query, w_key, w_value, w_out)
    return updated.reshape(members, ch, cols, lat)


def solution(mesh):
    return jax.shard_map(
        functools.partial(shards, mesh.shape["mem"], mesh.shape["lon"]),
        mesh=mesh,
        in_specs=(P("mem", None, "lon", None), P(), P(), P(), P()),
        out_specs=P("mem", None, "lon", None),
        check_vma=False,
    )
```

```python
import functools
import math

import jax
import jax.numpy as jnp
from jax import lax
from jax.experimental import pallas as pl
from jax.experimental.pallas import tpu as pltpu
from jax.sharding import PartitionSpec as P

MESH = pl.DeviceIdType.MESH
F32 = jnp.float32
BF16 = jnp.bfloat16


def with_halo(block, sides, width):
    for axis, dim in sides:
        count = lax.axis_size(axis)
        forward = [(i, i + 1) for i in range(count - 1)]
        forward.append((count - 1, 0))
        backward = [(target, source) for source, target in forward]
        low = lax.ppermute(
            lax.slice_in_dim(block, block.shape[dim] - width, None, axis=dim), axis, forward
        )
        high = lax.ppermute(lax.slice_in_dim(block, 0, width, axis=dim), axis, backward)
        block = jnp.concatenate([low, block, high], axis=dim)
    return block


def tap_stack(extended):
    span_lon = extended.shape[2] - 2
    latitudes = extended.shape[3]
    padded = jnp.pad(extended, ((0, 0), (0, 0), (0, 0), (1, 1)))
    return jnp.concatenate(
        [
            padded[:, :, lon_step : lon_step + span_lon, lat_step : lat_step + latitudes]
            for lon_step in range(3)
            for lat_step in range(3)
        ],
        axis=1,
    )


def plain_shards(fields, w_query, w_key, w_value, w_out):
    members = fields.shape[0]
    longitudes = fields.shape[2]
    latitudes = fields.shape[3]
    inner_width = w_query.shape[0]
    extended = with_halo(fields, (("lon", 2),), 1)
    w_inner = jnp.concatenate([w_query, w_key, w_value], axis=0)
    projected = jnp.einsum(
        "oc,mcwh->mowh", w_inner, tap_stack(extended), preferred_element_type=jnp.float32
    ).astype(jnp.bfloat16)
    queries = projected[:, :inner_width]
    keys_local = projected[:, inner_width : 2 * inner_width]
    values = projected[:, 2 * inner_width :]
    query_blocks, key_blocks = (
        lax.all_to_all(queries, "mem", split_axis=3, concat_axis=0, tiled=True),
        lax.all_to_all(keys_local, "mem", split_axis=3, concat_axis=0, tiled=True),
    )
    total_members = query_blocks.shape[0]
    partial_value = jnp.dot(
        query_blocks.reshape(total_members, -1),
        key_blocks.reshape(total_members, -1).T,
        preferred_element_type=jnp.float32,
    )
    score_scale = 1.0 / math.sqrt(inner_width * latitudes * longitudes * lax.axis_size("lon"))
    first_row = lax.axis_index("mem") * members
    gram_sums = lax.psum(partial_value, ("mem", "lon"))
    weights_all = jax.nn.softmax(gram_sums * score_scale, axis=1).astype(jnp.bfloat16)
    weights_own = lax.dynamic_slice_in_dim(weights_all, first_row, members, 0)
    mixed_values = jnp.einsum(
        "mn,ncwh->mcwh",
        weights_own,
        lax.all_gather(values, "mem", axis=0, tiled=True),
        preferred_element_type=jnp.float32,
    ).astype(jnp.bfloat16)
    mixed_ext = with_halo(mixed_values, (("lon", 2),), 1)
    branch = jnp.einsum(
        "oc,mcwh->mowh", w_out, tap_stack(mixed_ext), preferred_element_type=jnp.float32
    )
    return (fields.astype(jnp.float32) + branch).astype(jnp.bfloat16)


def lat_taps(block, lat):
    width = block.shape[1]
    lane = lax.broadcasted_iota(jnp.int32, block.shape, 1) & (lat - 1)
    low = jnp.where(lane == 0, 0.0, pltpu.roll(block, 1, 1))
    high = jnp.where(lane == lat - 1, 0.0, pltpu.roll(block, width - 1, 1))
    return jnp.concatenate([low, block, high], axis=0).astype(BF16)


def shifted_sum(taps_out, rows, lat):
    zero = jnp.zeros((rows, lat), F32)
    return (
        taps_out[rows : 2 * rows]
        + jnp.concatenate([zero, taps_out[:rows, :-lat]], axis=1)
        + jnp.concatenate([taps_out[2 * rows :, lat:], zero], axis=1)
    )


def layer_kernel(
    dims, f_ref, wq_ref, wk_ref, wv_ref, w_out_ref, out_ref,
    wi_ref, wo_ref, y_ref, halo, v_raw, qk_edge, qk_out, qk_all, v_all, g_out, g_mem, g_lon, edge_out, edge_in,
    halo_s, halo_r, qk_s, qk_r, v_s, v_r, gm_s, gm_r, gl_s, gl_r, edge_s, edge_r,
):
    mems, lons, members, ch, cq, cols, lat, score_scale = dims
    wide = cols * lat
    piece = wide // mems
    total = mems * members
    steps = cols // 2
    inner = 3 * cq
    z = lax.axis_index("mem")
    s = lax.axis_index("lon")
    right = lax.rem(s + 1, lons)
    left = lax.rem(s + lons - 1, lons)

    def mem_peer(d):
        return lax.rem(z + d, mems)

    def lon_peer(d):
        return lax.rem(s + d, lons)

    by_distance = [
        sorted([p for p in range(mems) if p != home], key=lambda p, home=home: (-abs(p - home), p))
        for home in range(mems)
    ]

    def far_peer(k):
        peer = by_distance[0][k]
        for home in range(1, mems):
            peer = jnp.where(z == home, by_distance[home][k], peer)
        return peer

    barrier = pltpu.get_barrier_semaphore()
    for d in range(1, mems):
        pl.semaphore_signal(barrier, inc=1, device_id={"mem": mem_peer(d)}, device_id_type=MESH)
    for d in range(1, lons):
        pl.semaphore_signal(barrier, inc=1, device_id={"lon": lon_peer(d)}, device_id_type=MESH)
    w_inner = jnp.concatenate([ref[...].astype(F32) for ref in (wq_ref, wk_ref, wv_ref)], axis=0)
    w_outer = w_out_ref[...].astype(F32)
    wi_ref[...] = jnp.concatenate([w_inner[:, a * 3 * ch : (a + 1) * 3 * ch] for a in range(3)], axis=0).astype(BF16)
    wo_ref[...] = jnp.concatenate([w_outer[:, a * 3 * cq : (a + 1) * 3 * cq] for a in range(3)], axis=0).astype(BF16)
    pl.semaphore_wait(barrier, mems + lons - 2)

    def remote(src, dst, send, recv, device):
        return pltpu.make_async_remote_copy(
            src_ref=src, dst_ref=dst, send_sem=send, recv_sem=recv, device_id=device, device_id_type=MESH
        )

    halo_copies = [
        remote(f_ref.at[:, :, pl.ds(wide - lat, lat)], halo.at[0], halo_s.at[0], halo_r.at[0], {"lon": right}),
        remote(f_ref.at[:, :, pl.ds(0, lat)], halo.at[1], halo_s.at[1], halo_r.at[1], {"lon": left}),
    ]
    for copy in halo_copies:
        copy.start()

    qk_copies = [remote(qk_out.at[p], qk_all.at[z], qk_s.at[p], qk_r.at[z], {"mem": p}) for p in range(mems)]
    for m in range(members):
        taps = lat_taps(f_ref[m].astype(F32), lat)
        projected = shifted_sum(jnp.dot(wi_ref[...], taps, preferred_element_type=F32), inner, lat)
        queries_keys = projected[: 2 * cq]
        v_raw[m] = projected[2 * cq :]
        qk_edge[0, m] = queries_keys[:, :lat]
        qk_edge[1, m] = queries_keys[:, wide - lat :]
        for p in range(mems):
            qk_out[p, m] = queries_keys[:, p * piece : (p + 1) * piece].astype(BF16)
        for p in range(1, mems - 1):
            @pl.when(z != p)
            def _(p=p, m=m):
                remote(qk_out.at[p, m], qk_all.at[z, m], qk_s.at[p], qk_r.at[z], {"mem": p}).start()
    for copy in halo_copies:
        copy.wait_recv()
    beside = []
    for side, rows in ((0, slice(0, inner)), (1, slice(2 * inner, 3 * inner))):
        columns = jnp.concatenate([halo[side, m] for m in range(members)], axis=1).astype(F32)
        beside.append(jnp.dot(wi_ref[rows], lat_taps(columns, lat), preferred_element_type=F32))
    for m in range(members):
        lanes = slice(m * lat, (m + 1) * lat)
        qk_out[0, m, :, :lat] = (qk_edge[0, m] + beside[0][: 2 * cq, lanes]).astype(BF16)
        qk_out[mems - 1, m, :, piece - lat :] = (qk_edge[1, m] + beside[1][: 2 * cq, lanes]).astype(BF16)
    for p in (0, mems - 1):
        @pl.when(z != p)
        def _(p=p):
            qk_copies[p].start()
    for m in range(members):
        lanes = slice(m * lat, (m + 1) * lat)
        for t in range(steps):
            upper = v_raw[m, :, t * lat : (t + 1) * lat]
            lower = v_raw[m, :, (steps + t) * lat : (steps + t + 1) * lat]
            if t == 0:
                upper = upper + beside[0][2 * cq :, lanes]
            if t == steps - 1:
                lower = lower + beside[1][2 * cq :, lanes]
            v_all[t, z, m] = jnp.concatenate([upper, lower], axis=0).astype(BF16)
    order = [0, steps - 1] + list(range(1, steps - 1))
    v_copies = {}
    for t in order:
        for k in range(mems - 1):
            v_copies[t, k] = remote(
                v_all.at[t, z], v_all.at[t, z], v_s.at[t, k], v_r.at[t, z], {"mem": far_peer(k)}
            )
    for k in range(mems - 1):
        peer = far_peer(k)
        remote(qk_out.at[peer], qk_all.at[z], qk_s.at[peer], qk_r.at[z], {"mem": peer}).wait_send()
        for t in order[:2]:
            v_copies[t, k].start()
    for t in order[2:]:
        for k in range(mems - 1):
            v_copies[t, k].start()

    qk_all[z] = qk_out[z]
    column = lax.broadcasted_iota(jnp.int32, (cq, total * cq), 1).astype(F32)
    row = lax.broadcasted_iota(jnp.int32, (cq, total * cq), 0).astype(F32)
    same = jnp.where(column - cq * jnp.floor((column + 0.5) / cq) == row, 1.0, 0.0)
    spread = lax.broadcasted_iota(jnp.int32, (total * cq, 128), 0) - cq * lax.broadcasted_iota(
        jnp.int32, (total * cq, 128), 1
    )
    groups = jnp.where((spread >= 0) & (spread < cq), 1.0, 0.0)
    for d in range(1, mems):
        source = mem_peer(d)
        remote(qk_out.at[source], qk_all.at[source], qk_s.at[source], qk_r.at[source], {"mem": source}).wait_recv()
    both = qk_all[...].astype(F32).reshape(total, 2 * cq, piece)
    queries = both[:, :cq].reshape(total * cq, piece).astype(BF16)
    keys = both[:, cq:].reshape(total * cq, piece).astype(BF16)
    products = lax.dot_general(queries, keys, (((1,), (1,)), ((), ())), preferred_element_type=F32)
    by_member = jnp.sum(products.reshape(total, cq, total * cq) * same[None], axis=1)
    gram = jnp.dot(by_member, groups, precision=lax.Precision.HIGHEST, preferred_element_type=F32)
    filler = jnp.zeros((8 - members, 128), F32)
    for p in range(mems):
        g_out[p] = jnp.concatenate([gram[p * members : (p + 1) * members], filler], axis=0)
    gm_copies = [
        remote(g_out.at[mem_peer(d)], g_mem.at[z], gm_s.at[d - 1], gm_r.at[d - 1], {"mem": mem_peer(d)})
        for d in range(1, mems)
    ]
    for copy in gm_copies:
        copy.start()
    g_mem[z] = g_out[z]
    for copy in gm_copies:
        copy.wait_recv()
    g_lon[s] = jnp.sum(g_mem[...], axis=0)
    gl_copies = [
        remote(g_lon.at[s], g_lon.at[s], gl_s.at[d - 1], gl_r.at[d - 1], {"lon": lon_peer(d)})
        for d in range(1, lons)
    ]
    for copy in gl_copies:
        copy.start()
    for copy in gl_copies:
        copy.wait_recv()
    lane = lax.broadcasted_iota(jnp.int32, (8, 128), 1)
    scores = jnp.where(lane < total, jnp.sum(g_lon[...], axis=0) * score_scale, -jnp.inf)
    powers = jnp.exp(scores - jnp.max(scores, axis=1, keepdims=True))
    weights = (powers / jnp.sum(powers, axis=1, keepdims=True)).astype(BF16).astype(F32)

    edge_copies = [
        remote(edge_out.at[0], edge_in.at[0], edge_s.at[0], edge_r.at[0], {"lon": right}),
        remote(edge_out.at[1], edge_in.at[1], edge_s.at[1], edge_r.at[1], {"lon": left}),
    ]
    edge_pad = jnp.zeros((edge_out.shape[2] - cq, lat), F32)
    for t in order:
        for d in range(1, mems):
            source = mem_peer(d)
            remote(v_all.at[t, source], v_all.at[t, source], v_s.at[t, 0], v_r.at[t, source], {"mem": source}).wait_recv()
        sums = [None] * members
        for n in range(total):
            block = v_all[t, n // members, n % members].astype(F32)
            for m in range(members):
                term = weights[m : m + 1, n : n + 1] * block
                sums[m] = term if n == 0 else sums[m] + term
        rounded = [sums[m].astype(BF16).astype(F32) for m in range(members)]
        if t == 0:
            for m in range(members):
                edge_out[1, m] = jnp.concatenate([rounded[m][:cq], edge_pad], axis=0).astype(BF16)
            edge_copies[1].start()
        if t == steps - 1:
            for m in range(members):
                edge_out[0, m] = jnp.concatenate([rounded[m][cq:], edge_pad], axis=0).astype(BF16)
            edge_copies[0].start()
        columns = jnp.concatenate([r[:cq] for r in rounded] + [r[cq:] for r in rounded], axis=1)
        y_ref[t] = jnp.dot(wo_ref[...], lat_taps(columns, lat), preferred_element_type=F32)
    for copy in edge_copies:
        copy.wait_recv()
    beside = []
    for side, rows in ((0, slice(0, ch)), (1, slice(2 * ch, 3 * ch))):
        columns = jnp.concatenate([edge_in[side, m].astype(F32)[:cq] for m in range(members)], axis=1)
        beside.append(jnp.dot(wo_ref[rows], lat_taps(columns, lat), preferred_element_type=F32))
    for m in range(members):
        def column_taps(tap, i):
            if i < 0 or i >= cols:
                return beside[0 if i < 0 else 1][:, m * lat : (m + 1) * lat]
            first = ((i // steps) * members + m) * lat
            return y_ref[i % steps, tap * ch : (tap + 1) * ch, first : first + lat]

        for i in range(cols):
            lanes = slice(i * lat, (i + 1) * lat)
            branch = column_taps(1, i) + column_taps(0, i - 1) + column_taps(2, i + 1)
            out_ref[m, :, lanes] = (f_ref[m, :, lanes].astype(F32) + branch).astype(BF16)
    for copy in halo_copies + list(v_copies.values()) + gm_copies + gl_copies + edge_copies:
        copy.wait_send()


def shards(mems, lons, fields, w_query, w_key, w_value, w_out):
    members, ch, cols, lat = fields.shape
    cq = w_query.shape[0]
    wide = cols * lat
    if cols % mems or cols % 2 or cols < 4 or mems < 2 or lat != 128 or members > 8 or (2 * cq) % 16 or ch % 16:
        return plain_shards(fields, w_query, w_key, w_value, w_out)
    score_scale = 1.0 / math.sqrt(cq * lat * cols * lons)
    dims = (mems, lons, members, ch, cq, cols, lat, score_scale)
    edge_rows = -(-cq // 16) * 16
    dma = pltpu.SemaphoreType.DMA
    vmem = pl.BlockSpec(memory_space=pltpu.VMEM)
    updated = pl.pallas_call(
        functools.partial(layer_kernel, dims),
        out_shape=jax.ShapeDtypeStruct((members, ch, wide), BF16),
        in_specs=[vmem] * 5,
        out_specs=vmem,
        scratch_shapes=[
            pltpu.VMEM((9 * cq, 3 * ch), BF16),
            pltpu.VMEM((3 * ch, 3 * cq), BF16),
            pltpu.VMEM((cols // 2, 3 * ch, 2 * members * lat), F32),
            pltpu.VMEM((2, members, ch, lat), BF16),
            pltpu.VMEM((members, cq, wide), F32),
            pltpu.VMEM((2, members, 2 * cq, lat), F32),
            pltpu.VMEM((mems, members, 2 * cq, wide // mems), BF16),
            pltpu.VMEM((mems, members, 2 * cq, wide // mems), BF16),
            pltpu.VMEM((cols // 2, mems, members, 2 * cq, lat), BF16),
            pltpu.VMEM((mems, 8, 128), F32),
            pltpu.VMEM((mems, 8, 128), F32),
            pltpu.VMEM((lons, 8, 128), F32),
            pltpu.VMEM((2, members, edge_rows, lat), BF16),
            pltpu.VMEM((2, members, edge_rows, lat), BF16),
            dma((2,)), dma((2,)),
            dma((mems,)), dma((mems,)),
            dma((cols // 2, mems - 1)), dma((cols // 2, mems)),
            dma((mems - 1,)), dma((mems - 1,)),
            dma((lons - 1,)), dma((lons - 1,)),
            dma((2,)), dma((2,)),
        ],
        compiler_params=pltpu.CompilerParams(
            collective_id=0, has_side_effects=True, vmem_limit_bytes=40 * 1024 * 1024
        ),
    )(fields.reshape(members, ch, wide), w_query, w_key, w_value, w_out)
    return updated.reshape(members, ch, cols, lat)


def solution(mesh):
    return jax.shard_map(
        functools.partial(shards, mesh.shape["mem"], mesh.shape["lon"]),
        mesh=mesh,
        in_specs=(P("mem", None, "lon", None), P(), P(), P(), P()),
        out_specs=P("mem", None, "lon", None),
        check_vma=False,
    )
```

```python
import functools
import math

import jax
import jax.numpy as jnp
from jax import lax
from jax.experimental import pallas as pl
from jax.experimental.pallas import tpu as pltpu
from jax.sharding import PartitionSpec as P

MESH = pl.DeviceIdType.MESH
F32 = jnp.float32
BF16 = jnp.bfloat16


def with_halo(block, sides, width):
    for axis, dim in sides:
        count = lax.axis_size(axis)
        forward = [(i, i + 1) for i in range(count - 1)]
        forward.append((count - 1, 0))
        backward = [(target, source) for source, target in forward]
        low = lax.ppermute(
            lax.slice_in_dim(block, block.shape[dim] - width, None, axis=dim), axis, forward
        )
        high = lax.ppermute(lax.slice_in_dim(block, 0, width, axis=dim), axis, backward)
        block = jnp.concatenate([low, block, high], axis=dim)
    return block


def tap_stack(extended):
    span_lon = extended.shape[2] - 2
    latitudes = extended.shape[3]
    padded = jnp.pad(extended, ((0, 0), (0, 0), (0, 0), (1, 1)))
    return jnp.concatenate(
        [
            padded[:, :, lon_step : lon_step + span_lon, lat_step : lat_step + latitudes]
            for lon_step in range(3)
            for lat_step in range(3)
        ],
        axis=1,
    )


def plain_shards(fields, w_query, w_key, w_value, w_out):
    members = fields.shape[0]
    longitudes = fields.shape[2]
    latitudes = fields.shape[3]
    inner_width = w_query.shape[0]
    extended = with_halo(fields, (("lon", 2),), 1)
    w_inner = jnp.concatenate([w_query, w_key, w_value], axis=0)
    projected = jnp.einsum(
        "oc,mcwh->mowh", w_inner, tap_stack(extended), preferred_element_type=jnp.float32
    ).astype(jnp.bfloat16)
    queries = projected[:, :inner_width]
    keys_local = projected[:, inner_width : 2 * inner_width]
    values = projected[:, 2 * inner_width :]
    query_blocks, key_blocks = (
        lax.all_to_all(queries, "mem", split_axis=3, concat_axis=0, tiled=True),
        lax.all_to_all(keys_local, "mem", split_axis=3, concat_axis=0, tiled=True),
    )
    total_members = query_blocks.shape[0]
    partial_value = jnp.dot(
        query_blocks.reshape(total_members, -1),
        key_blocks.reshape(total_members, -1).T,
        preferred_element_type=jnp.float32,
    )
    score_scale = 1.0 / math.sqrt(inner_width * latitudes * longitudes * lax.axis_size("lon"))
    first_row = lax.axis_index("mem") * members
    gram_sums = lax.psum(partial_value, ("mem", "lon"))
    weights_all = jax.nn.softmax(gram_sums * score_scale, axis=1).astype(jnp.bfloat16)
    weights_own = lax.dynamic_slice_in_dim(weights_all, first_row, members, 0)
    mixed_values = jnp.einsum(
        "mn,ncwh->mcwh",
        weights_own,
        lax.all_gather(values, "mem", axis=0, tiled=True),
        preferred_element_type=jnp.float32,
    ).astype(jnp.bfloat16)
    mixed_ext = with_halo(mixed_values, (("lon", 2),), 1)
    branch = jnp.einsum(
        "oc,mcwh->mowh", w_out, tap_stack(mixed_ext), preferred_element_type=jnp.float32
    )
    return (fields.astype(jnp.float32) + branch).astype(jnp.bfloat16)


def lat_taps(block, lat):
    width = block.shape[1]
    lane = lax.broadcasted_iota(jnp.int32, block.shape, 1) & (lat - 1)
    low = jnp.where(lane == 0, 0.0, pltpu.roll(block, 1, 1))
    high = jnp.where(lane == lat - 1, 0.0, pltpu.roll(block, width - 1, 1))
    return jnp.concatenate([low, block, high], axis=0).astype(BF16)


def shifted_sum(taps_out, rows, lat):
    zero = jnp.zeros((rows, lat), F32)
    return (
        taps_out[rows : 2 * rows]
        + jnp.concatenate([zero, taps_out[:rows, :-lat]], axis=1)
        + jnp.concatenate([taps_out[2 * rows :, lat:], zero], axis=1)
    )


def layer_kernel(
    dims, f_ref, wq_ref, wk_ref, wv_ref, w_out_ref, out_ref,
    wi_ref, wo_ref, y_ref, halo, v_raw, qk_edge, qk_out, qk_all, v_all, g_out, g_mem, g_lon, edge_out, edge_in,
    halo_s, halo_r, qk_s, qk_r, v_s, v_r, gm_s, gm_r, gl_s, gl_r, edge_s, edge_r,
):
    mems, lons, members, ch, cq, cols, lat, score_scale = dims
    wide = cols * lat
    piece = wide // mems
    total = mems * members
    steps = cols // 2
    inner = 3 * cq
    z = lax.axis_index("mem")
    s = lax.axis_index("lon")
    right = lax.rem(s + 1, lons)
    left = lax.rem(s + lons - 1, lons)

    def mem_peer(d):
        return lax.rem(z + d, mems)

    def lon_peer(d):
        return lax.rem(s + d, lons)

    by_distance = [
        sorted([p for p in range(mems) if p != home], key=lambda p, home=home: (-abs(p - home), p))
        for home in range(mems)
    ]

    def far_peer(k):
        peer = by_distance[0][k]
        for home in range(1, mems):
            peer = jnp.where(z == home, by_distance[home][k], peer)
        return peer

    barrier = pltpu.get_barrier_semaphore()
    for d in range(1, mems):
        pl.semaphore_signal(barrier, inc=1, device_id={"mem": mem_peer(d)}, device_id_type=MESH)
    for d in range(1, lons):
        pl.semaphore_signal(barrier, inc=1, device_id={"lon": lon_peer(d)}, device_id_type=MESH)
    w_inner = jnp.concatenate([ref[...].astype(F32) for ref in (wq_ref, wk_ref, wv_ref)], axis=0)
    w_outer = w_out_ref[...].astype(F32)
    wi_ref[...] = jnp.concatenate([w_inner[:, a * 3 * ch : (a + 1) * 3 * ch] for a in range(3)], axis=0).astype(BF16)
    wo_ref[...] = jnp.concatenate([w_outer[:, a * 3 * cq : (a + 1) * 3 * cq] for a in range(3)], axis=0).astype(BF16)
    pl.semaphore_wait(barrier, mems + lons - 2)

    def remote(src, dst, send, recv, device):
        return pltpu.make_async_remote_copy(
            src_ref=src, dst_ref=dst, send_sem=send, recv_sem=recv, device_id=device, device_id_type=MESH
        )

    halo_copies = [
        remote(f_ref.at[:, :, pl.ds(wide - lat, lat)], halo.at[0], halo_s.at[0], halo_r.at[0], {"lon": right}),
        remote(f_ref.at[:, :, pl.ds(0, lat)], halo.at[1], halo_s.at[1], halo_r.at[1], {"lon": left}),
    ]
    for copy in halo_copies:
        copy.start()

    qk_copies = [remote(qk_out.at[p], qk_all.at[z], qk_s.at[p], qk_r.at[z], {"mem": p}) for p in range(mems)]
    for m in range(members):
        taps = lat_taps(f_ref[m].astype(F32), lat)
        projected = shifted_sum(jnp.dot(wi_ref[...], taps, preferred_element_type=F32), inner, lat)
        queries_keys = projected[: 2 * cq]
        v_raw[m] = projected[2 * cq :]
        qk_edge[0, m] = queries_keys[:, :lat]
        qk_edge[1, m] = queries_keys[:, wide - lat :]
        for p in range(mems):
            qk_out[p, m] = queries_keys[:, p * piece : (p + 1) * piece].astype(BF16)
        for p in range(1, mems - 1):
            @pl.when(z != p)
            def _(p=p, m=m):
                remote(qk_out.at[p, m], qk_all.at[z, m], qk_s.at[p], qk_r.at[z], {"mem": p}).start()
    for copy in halo_copies:
        copy.wait_recv()
    beside = []
    for side, rows in ((0, slice(0, inner)), (1, slice(2 * inner, 3 * inner))):
        columns = jnp.concatenate([halo[side, m] for m in range(members)], axis=1).astype(F32)
        beside.append(jnp.dot(wi_ref[rows], lat_taps(columns, lat), preferred_element_type=F32))
    for m in range(members):
        lanes = slice(m * lat, (m + 1) * lat)
        qk_out[0, m, :, :lat] = (qk_edge[0, m] + beside[0][: 2 * cq, lanes]).astype(BF16)
        qk_out[mems - 1, m, :, piece - lat :] = (qk_edge[1, m] + beside[1][: 2 * cq, lanes]).astype(BF16)
    for p in (0, mems - 1):
        @pl.when(z != p)
        def _(p=p):
            qk_copies[p].start()
    for m in range(members):
        lanes = slice(m * lat, (m + 1) * lat)
        for t in range(steps):
            upper = v_raw[m, :, t * lat : (t + 1) * lat]
            lower = v_raw[m, :, (steps + t) * lat : (steps + t + 1) * lat]
            if t == 0:
                upper = upper + beside[0][2 * cq :, lanes]
            if t == steps - 1:
                lower = lower + beside[1][2 * cq :, lanes]
            v_all[t, z, m] = jnp.concatenate([upper, lower], axis=0).astype(BF16)
    order = [0, steps - 1] + list(range(1, steps - 1))
    v_copies = {}
    for t in order:
        for k in range(mems - 1):
            v_copies[t, k] = remote(
                v_all.at[t, z], v_all.at[t, z], v_s.at[t, k], v_r.at[t, z], {"mem": far_peer(k)}
            )
    for k in range(mems - 1):
        peer = far_peer(k)
        remote(qk_out.at[peer], qk_all.at[z], qk_s.at[peer], qk_r.at[z], {"mem": peer}).wait_send()
        v_copies[order[0], k].start()

    qk_all[z] = qk_out[z]
    column = lax.broadcasted_iota(jnp.int32, (cq, total * cq), 1).astype(F32)
    row = lax.broadcasted_iota(jnp.int32, (cq, total * cq), 0).astype(F32)
    same = jnp.where(column - cq * jnp.floor((column + 0.5) / cq) == row, 1.0, 0.0)
    spread = lax.broadcasted_iota(jnp.int32, (total * cq, 128), 0) - cq * lax.broadcasted_iota(
        jnp.int32, (total * cq, 128), 1
    )
    groups = jnp.where((spread >= 0) & (spread < cq), 1.0, 0.0)
    for d in range(1, mems):
        source = mem_peer(d)
        remote(qk_out.at[source], qk_all.at[source], qk_s.at[source], qk_r.at[source], {"mem": source}).wait_recv()
    both = qk_all[...].astype(F32).reshape(total, 2 * cq, piece)
    queries = both[:, :cq].reshape(total * cq, piece).astype(BF16)
    keys = both[:, cq:].reshape(total * cq, piece).astype(BF16)
    products = lax.dot_general(queries, keys, (((1,), (1,)), ((), ())), preferred_element_type=F32)
    by_member = jnp.sum(products.reshape(total, cq, total * cq) * same[None], axis=1)
    gram = jnp.dot(by_member, groups, precision=lax.Precision.HIGHEST, preferred_element_type=F32)
    filler = jnp.zeros((8 - members, 128), F32)
    for p in range(mems):
        g_out[p] = jnp.concatenate([gram[p * members : (p + 1) * members], filler], axis=0)
    gm_copies = [
        remote(g_out.at[mem_peer(d)], g_mem.at[z], gm_s.at[d - 1], gm_r.at[d - 1], {"mem": mem_peer(d)})
        for d in range(1, mems)
    ]
    for copy in gm_copies:
        copy.start()
    for t in order[1:]:
        for k in range(mems - 1):
            v_copies[t, k].start()
    g_mem[z] = g_out[z]
    for copy in gm_copies:
        copy.wait_recv()
    g_lon[s] = jnp.sum(g_mem[...], axis=0)
    gl_copies = [
        remote(g_lon.at[s], g_lon.at[s], gl_s.at[d - 1], gl_r.at[d - 1], {"lon": lon_peer(d)})
        for d in range(1, lons)
    ]
    for copy in gl_copies:
        copy.start()
    for copy in gl_copies:
        copy.wait_recv()
    lane = lax.broadcasted_iota(jnp.int32, (8, 128), 1)
    scores = jnp.where(lane < total, jnp.sum(g_lon[...], axis=0) * score_scale, -jnp.inf)
    powers = jnp.exp(scores - jnp.max(scores, axis=1, keepdims=True))
    weights = (powers / jnp.sum(powers, axis=1, keepdims=True)).astype(BF16).astype(F32)

    edge_copies = [
        remote(edge_out.at[0], edge_in.at[0], edge_s.at[0], edge_r.at[0], {"lon": right}),
        remote(edge_out.at[1], edge_in.at[1], edge_s.at[1], edge_r.at[1], {"lon": left}),
    ]
    edge_pad = jnp.zeros((edge_out.shape[2] - cq, lat), F32)
    for t in order:
        for d in range(1, mems):
            source = mem_peer(d)
            remote(v_all.at[t, source], v_all.at[t, source], v_s.at[t, 0], v_r.at[t, source], {"mem": source}).wait_recv()
        sums = [None] * members
        for n in range(total):
            block = v_all[t, n // members, n % members].astype(F32)
            for m in range(members):
                term = weights[m : m + 1, n : n + 1] * block
                sums[m] = term if n == 0 else sums[m] + term
        rounded = [sums[m].astype(BF16).astype(F32) for m in range(members)]
        if t == 0:
            for m in range(members):
                edge_out[1, m] = jnp.concatenate([rounded[m][:cq], edge_pad], axis=0).astype(BF16)
            edge_copies[1].start()
        if t == steps - 1:
            for m in range(members):
                edge_out[0, m] = jnp.concatenate([rounded[m][cq:], edge_pad], axis=0).astype(BF16)
            edge_copies[0].start()
        columns = jnp.concatenate([r[:cq] for r in rounded] + [r[cq:] for r in rounded], axis=1)
        y_ref[t] = jnp.dot(wo_ref[...], lat_taps(columns, lat), preferred_element_type=F32)
    for copy in edge_copies:
        copy.wait_recv()
    beside = []
    for side, rows in ((0, slice(0, ch)), (1, slice(2 * ch, 3 * ch))):
        columns = jnp.concatenate([edge_in[side, m].astype(F32)[:cq] for m in range(members)], axis=1)
        beside.append(jnp.dot(wo_ref[rows], lat_taps(columns, lat), preferred_element_type=F32))
    for m in range(members):
        def column_taps(tap, i):
            if i < 0 or i >= cols:
                return beside[0 if i < 0 else 1][:, m * lat : (m + 1) * lat]
            first = ((i // steps) * members + m) * lat
            return y_ref[i % steps, tap * ch : (tap + 1) * ch, first : first + lat]

        for i in range(cols):
            lanes = slice(i * lat, (i + 1) * lat)
            branch = column_taps(1, i) + column_taps(0, i - 1) + column_taps(2, i + 1)
            out_ref[m, :, lanes] = (f_ref[m, :, lanes].astype(F32) + branch).astype(BF16)
    for copy in halo_copies + list(v_copies.values()) + gm_copies + gl_copies + edge_copies:
        copy.wait_send()


def shards(mems, lons, fields, w_query, w_key, w_value, w_out):
    members, ch, cols, lat = fields.shape
    cq = w_query.shape[0]
    wide = cols * lat
    if cols % mems or cols % 2 or cols < 4 or mems < 2 or lat != 128 or members > 8 or (2 * cq) % 16 or ch % 16:
        return plain_shards(fields, w_query, w_key, w_value, w_out)
    score_scale = 1.0 / math.sqrt(cq * lat * cols * lons)
    dims = (mems, lons, members, ch, cq, cols, lat, score_scale)
    edge_rows = -(-cq // 16) * 16
    dma = pltpu.SemaphoreType.DMA
    vmem = pl.BlockSpec(memory_space=pltpu.VMEM)
    updated = pl.pallas_call(
        functools.partial(layer_kernel, dims),
        out_shape=jax.ShapeDtypeStruct((members, ch, wide), BF16),
        in_specs=[vmem] * 5,
        out_specs=vmem,
        scratch_shapes=[
            pltpu.VMEM((9 * cq, 3 * ch), BF16),
            pltpu.VMEM((3 * ch, 3 * cq), BF16),
            pltpu.VMEM((cols // 2, 3 * ch, 2 * members * lat), F32),
            pltpu.VMEM((2, members, ch, lat), BF16),
            pltpu.VMEM((members, cq, wide), F32),
            pltpu.VMEM((2, members, 2 * cq, lat), F32),
            pltpu.VMEM((mems, members, 2 * cq, wide // mems), BF16),
            pltpu.VMEM((mems, members, 2 * cq, wide // mems), BF16),
            pltpu.VMEM((cols // 2, mems, members, 2 * cq, lat), BF16),
            pltpu.VMEM((mems, 8, 128), F32),
            pltpu.VMEM((mems, 8, 128), F32),
            pltpu.VMEM((lons, 8, 128), F32),
            pltpu.VMEM((2, members, edge_rows, lat), BF16),
            pltpu.VMEM((2, members, edge_rows, lat), BF16),
            dma((2,)), dma((2,)),
            dma((mems,)), dma((mems,)),
            dma((cols // 2, mems - 1)), dma((cols // 2, mems)),
            dma((mems - 1,)), dma((mems - 1,)),
            dma((lons - 1,)), dma((lons - 1,)),
            dma((2,)), dma((2,)),
        ],
        compiler_params=pltpu.CompilerParams(
            collective_id=0, has_side_effects=True, vmem_limit_bytes=40 * 1024 * 1024
        ),
    )(fields.reshape(members, ch, wide), w_query, w_key, w_value, w_out)
    return updated.reshape(members, ch, cols, lat)


def solution(mesh):
    return jax.shard_map(
        functools.partial(shards, mesh.shape["mem"], mesh.shape["lon"]),
        mesh=mesh,
        in_specs=(P("mem", None, "lon", None), P(), P(), P(), P()),
        out_specs=P("mem", None, "lon", None),
        check_vma=False,
    )
```

```python
import functools
import math

import jax
import jax.numpy as jnp
from jax import lax
from jax.experimental import pallas as pl
from jax.experimental.pallas import tpu as pltpu
from jax.sharding import PartitionSpec as P

MESH = pl.DeviceIdType.MESH
F32 = jnp.float32
BF16 = jnp.bfloat16


def with_halo(block, sides, width):
    for axis, dim in sides:
        count = lax.axis_size(axis)
        forward = [(i, i + 1) for i in range(count - 1)]
        forward.append((count - 1, 0))
        backward = [(target, source) for source, target in forward]
        low = lax.ppermute(
            lax.slice_in_dim(block, block.shape[dim] - width, None, axis=dim), axis, forward
        )
        high = lax.ppermute(lax.slice_in_dim(block, 0, width, axis=dim), axis, backward)
        block = jnp.concatenate([low, block, high], axis=dim)
    return block


def tap_stack(extended):
    span_lon = extended.shape[2] - 2
    latitudes = extended.shape[3]
    padded = jnp.pad(extended, ((0, 0), (0, 0), (0, 0), (1, 1)))
    return jnp.concatenate(
        [
            padded[:, :, lon_step : lon_step + span_lon, lat_step : lat_step + latitudes]
            for lon_step in range(3)
            for lat_step in range(3)
        ],
        axis=1,
    )


def plain_shards(fields, w_query, w_key, w_value, w_out):
    members = fields.shape[0]
    longitudes = fields.shape[2]
    latitudes = fields.shape[3]
    inner_width = w_query.shape[0]
    extended = with_halo(fields, (("lon", 2),), 1)
    w_inner = jnp.concatenate([w_query, w_key, w_value], axis=0)
    projected = jnp.einsum(
        "oc,mcwh->mowh", w_inner, tap_stack(extended), preferred_element_type=jnp.float32
    ).astype(jnp.bfloat16)
    queries = projected[:, :inner_width]
    keys_local = projected[:, inner_width : 2 * inner_width]
    values = projected[:, 2 * inner_width :]
    query_blocks, key_blocks = (
        lax.all_to_all(queries, "mem", split_axis=3, concat_axis=0, tiled=True),
        lax.all_to_all(keys_local, "mem", split_axis=3, concat_axis=0, tiled=True),
    )
    total_members = query_blocks.shape[0]
    partial_value = jnp.dot(
        query_blocks.reshape(total_members, -1),
        key_blocks.reshape(total_members, -1).T,
        preferred_element_type=jnp.float32,
    )
    score_scale = 1.0 / math.sqrt(inner_width * latitudes * longitudes * lax.axis_size("lon"))
    first_row = lax.axis_index("mem") * members
    gram_sums = lax.psum(partial_value, ("mem", "lon"))
    weights_all = jax.nn.softmax(gram_sums * score_scale, axis=1).astype(jnp.bfloat16)
    weights_own = lax.dynamic_slice_in_dim(weights_all, first_row, members, 0)
    mixed_values = jnp.einsum(
        "mn,ncwh->mcwh",
        weights_own,
        lax.all_gather(values, "mem", axis=0, tiled=True),
        preferred_element_type=jnp.float32,
    ).astype(jnp.bfloat16)
    mixed_ext = with_halo(mixed_values, (("lon", 2),), 1)
    branch = jnp.einsum(
        "oc,mcwh->mowh", w_out, tap_stack(mixed_ext), preferred_element_type=jnp.float32
    )
    return (fields.astype(jnp.float32) + branch).astype(jnp.bfloat16)


def lat_taps(block, lat):
    width = block.shape[1]
    lane = lax.broadcasted_iota(jnp.int32, block.shape, 1) & (lat - 1)
    low = jnp.where(lane == 0, 0.0, pltpu.roll(block, 1, 1))
    high = jnp.where(lane == lat - 1, 0.0, pltpu.roll(block, width - 1, 1))
    return jnp.concatenate([low, block, high], axis=0).astype(BF16)


def shifted_sum(taps_out, rows, lat):
    zero = jnp.zeros((rows, lat), F32)
    return (
        taps_out[rows : 2 * rows]
        + jnp.concatenate([zero, taps_out[:rows, :-lat]], axis=1)
        + jnp.concatenate([taps_out[2 * rows :, lat:], zero], axis=1)
    )


def layer_kernel(
    dims, f_ref, wq_ref, wk_ref, wv_ref, w_out_ref, out_ref,
    wi_ref, wo_ref, y_ref, halo, v_raw, qk_edge, by_member, qk_out, qk_all, v_all, g_out, g_mem, g_lon, edge_out, edge_in,
    halo_s, halo_r, qk_s, qk_r, v_s, v_r, gm_s, gm_r, gl_s, gl_r, edge_s, edge_r,
):
    mems, lons, members, ch, cq, cols, lat, score_scale = dims
    wide = cols * lat
    slots = cols // 2 - 1
    is_inner = (lax.axis_index("mem") > 0) & (lax.axis_index("mem") < mems - 1)
    total = mems * members
    steps = cols // 2
    inner = 3 * cq
    z = lax.axis_index("mem")
    s = lax.axis_index("lon")
    right = lax.rem(s + 1, lons)
    left = lax.rem(s + lons - 1, lons)

    def mem_peer(d):
        return lax.rem(z + d, mems)

    def lon_peer(d):
        return lax.rem(s + d, lons)

    by_distance = [
        sorted([p for p in range(mems) if p != home], key=lambda p, home=home: (-abs(p - home), p))
        for home in range(mems)
    ]

    def far_peer(k):
        peer = by_distance[0][k]
        for home in range(1, mems):
            peer = jnp.where(z == home, by_distance[home][k], peer)
        return peer

    barrier = pltpu.get_barrier_semaphore()
    for d in range(1, mems):
        pl.semaphore_signal(barrier, inc=1, device_id={"mem": mem_peer(d)}, device_id_type=MESH)
    for d in range(1, lons):
        pl.semaphore_signal(barrier, inc=1, device_id={"lon": lon_peer(d)}, device_id_type=MESH)
    w_inner = jnp.concatenate([ref[...].astype(F32) for ref in (wq_ref, wk_ref, wv_ref)], axis=0)
    w_outer = w_out_ref[...].astype(F32)
    wi_ref[...] = jnp.concatenate([w_inner[:, a * 3 * ch : (a + 1) * 3 * ch] for a in range(3)], axis=0).astype(BF16)
    wo_ref[...] = jnp.concatenate([w_outer[:, a * 3 * cq : (a + 1) * 3 * cq] for a in range(3)], axis=0).astype(BF16)
    pl.semaphore_wait(barrier, mems + lons - 2)

    def remote(src, dst, send, recv, device):
        return pltpu.make_async_remote_copy(
            src_ref=src, dst_ref=dst, send_sem=send, recv_sem=recv, device_id=device, device_id_type=MESH
        )

    halo_copies = [
        remote(f_ref.at[:, :, pl.ds(wide - lat, lat)], halo.at[0], halo_s.at[0], halo_r.at[0], {"lon": right}),
        remote(f_ref.at[:, :, pl.ds(0, lat)], halo.at[1], halo_s.at[1], halo_r.at[1], {"lon": left}),
    ]
    for copy in halo_copies:
        copy.start()

    def qk_copy(p):
        if 0 < p < mems - 1:
            return remote(qk_out.at[p], qk_all.at[z], qk_s.at[p], qk_r.at[z], {"mem": p})
        return remote(qk_out.at[p, 0], qk_all.at[z, 0], qk_s.at[p], qk_r.at[z], {"mem": p})

    for m in range(members):
        taps = lat_taps(f_ref[m].astype(F32), lat)
        projected = shifted_sum(jnp.dot(wi_ref[...], taps, preferred_element_type=F32), inner, lat)
        queries_keys = projected[: 2 * cq]
        v_raw[m] = projected[2 * cq :]
        qk_edge[0, m] = queries_keys[:, :lat]
        qk_edge[1, m] = queries_keys[:, wide - lat :]
        for i in range(1, cols - 1):
            qk_out[1 + (i - 1) // slots, (i - 1) % slots, m] = queries_keys[:, i * lat : (i + 1) * lat].astype(BF16)
        for p in range(1, mems - 1):
            @pl.when(z != p)
            def _(p=p, m=m):
                remote(qk_out.at[p, :, m], qk_all.at[z, :, m], qk_s.at[p], qk_r.at[z], {"mem": p}).start()
    for copy in halo_copies:
        copy.wait_recv()
    beside = []
    for side, rows in ((0, slice(0, inner)), (1, slice(2 * inner, 3 * inner))):
        columns = jnp.concatenate([halo[side, m] for m in range(members)], axis=1).astype(F32)
        beside.append(jnp.dot(wi_ref[rows], lat_taps(columns, lat), preferred_element_type=F32))
    for m in range(members):
        lanes = slice(m * lat, (m + 1) * lat)
        qk_out[0, 0, m] = (qk_edge[0, m] + beside[0][: 2 * cq, lanes]).astype(BF16)
        qk_out[mems - 1, 0, m] = (qk_edge[1, m] + beside[1][: 2 * cq, lanes]).astype(BF16)
    for p in (0, mems - 1):
        @pl.when(z != p)
        def _(p=p):
            qk_copy(p).start()
    for m in range(members):
        lanes = slice(m * lat, (m + 1) * lat)
        for t in range(steps):
            upper = v_raw[m, :, t * lat : (t + 1) * lat]
            lower = v_raw[m, :, (steps + t) * lat : (steps + t + 1) * lat]
            if t == 0:
                upper = upper + beside[0][2 * cq :, lanes]
            if t == steps - 1:
                lower = lower + beside[1][2 * cq :, lanes]
            v_all[t, z, m] = jnp.concatenate([upper, lower], axis=0).astype(BF16)
    order = [0, steps - 1] + list(range(1, steps - 1))
    v_copies = {}
    for t in order:
        for k in range(mems - 1):
            v_copies[t, k] = remote(
                v_all.at[t, z], v_all.at[t, z], v_s.at[t, k], v_r.at[t, z], {"mem": far_peer(k)}
            )
    for k in range(mems - 1):
        v_copies[order[0], k].start()

    column = lax.broadcasted_iota(jnp.int32, (cq, total * cq), 1).astype(F32)
    row = lax.broadcasted_iota(jnp.int32, (cq, total * cq), 0).astype(F32)
    same = jnp.where(column - cq * jnp.floor((column + 0.5) / cq) == row, 1.0, 0.0)
    spread = lax.broadcasted_iota(jnp.int32, (total * cq, 128), 0) - cq * lax.broadcasted_iota(
        jnp.int32, (total * cq, 128), 1
    )
    groups = jnp.where((spread >= 0) & (spread < cq), 1.0, 0.0)
    def add_columns(first, count):
        parts = [qk_all[:, first + j].astype(F32).reshape(total, 2 * cq, lat) for j in range(count)]
        both = jnp.concatenate(parts, axis=2)
        queries = both[:, :cq].reshape(total * cq, count * lat).astype(BF16)
        keys = both[:, cq:].reshape(total * cq, count * lat).astype(BF16)
        products = lax.dot_general(queries, keys, (((1,), (1,)), ((), ())), preferred_element_type=F32)
        return jnp.sum(products.reshape(total, cq, total * cq) * same[None], axis=1)

    @pl.when(is_inner)
    def _():
        qk_all[z] = qk_out[z]
        for d in range(1, mems):
            source = mem_peer(d)
            remote(qk_out.at[source], qk_all.at[source], qk_s.at[0], qk_r.at[source], {"mem": source}).wait_recv()
        by_member[...] = add_columns(0, slots)

    @pl.when(jnp.logical_not(is_inner))
    def _():
        qk_all[z, 0] = qk_out[z, 0]
        for d in range(1, mems):
            source = mem_peer(d)
            remote(
                qk_out.at[source, 0], qk_all.at[source, 0], qk_s.at[0], qk_r.at[source], {"mem": source}
            ).wait_recv()
        by_member[...] = add_columns(0, 1)

    gram = jnp.dot(by_member[...], groups, precision=lax.Precision.HIGHEST, preferred_element_type=F32)
    filler = jnp.zeros((8 - members, 128), F32)
    for p in range(mems):
        g_out[p] = jnp.concatenate([gram[p * members : (p + 1) * members], filler], axis=0)
    gm_copies = [
        remote(g_out.at[mem_peer(d)], g_mem.at[z], gm_s.at[d - 1], gm_r.at[d - 1], {"mem": mem_peer(d)})
        for d in range(1, mems)
    ]
    for copy in gm_copies:
        copy.start()
    for t in order[1:]:
        for k in range(mems - 1):
            v_copies[t, k].start()
    g_mem[z] = g_out[z]
    for copy in gm_copies:
        copy.wait_recv()
    g_lon[s] = jnp.sum(g_mem[...], axis=0)
    gl_copies = [
        remote(g_lon.at[s], g_lon.at[s], gl_s.at[d - 1], gl_r.at[d - 1], {"lon": lon_peer(d)})
        for d in range(1, lons)
    ]
    for copy in gl_copies:
        copy.start()
    for copy in gl_copies:
        copy.wait_recv()
    lane = lax.broadcasted_iota(jnp.int32, (8, 128), 1)
    scores = jnp.where(lane < total, jnp.sum(g_lon[...], axis=0) * score_scale, -jnp.inf)
    powers = jnp.exp(scores - jnp.max(scores, axis=1, keepdims=True))
    weights = (powers / jnp.sum(powers, axis=1, keepdims=True)).astype(BF16).astype(F32)

    edge_copies = [
        remote(edge_out.at[0], edge_in.at[0], edge_s.at[0], edge_r.at[0], {"lon": right}),
        remote(edge_out.at[1], edge_in.at[1], edge_s.at[1], edge_r.at[1], {"lon": left}),
    ]
    edge_pad = jnp.zeros((edge_out.shape[2] - cq, lat), F32)
    for t in order:
        for d in range(1, mems):
            source = mem_peer(d)
            remote(v_all.at[t, source], v_all.at[t, source], v_s.at[t, 0], v_r.at[t, source], {"mem": source}).wait_recv()
        sums = [None] * members
        for n in range(total):
            block = v_all[t, n // members, n % members].astype(F32)
            for m in range(members):
                term = weights[m : m + 1, n : n + 1] * block
                sums[m] = term if n == 0 else sums[m] + term
        rounded = [sums[m].astype(BF16).astype(F32) for m in range(members)]
        if t == 0:
            for m in range(members):
                edge_out[1, m] = jnp.concatenate([rounded[m][:cq], edge_pad], axis=0).astype(BF16)
            edge_copies[1].start()
        if t == steps - 1:
            for m in range(members):
                edge_out[0, m] = jnp.concatenate([rounded[m][cq:], edge_pad], axis=0).astype(BF16)
            edge_copies[0].start()
        columns = jnp.concatenate([r[:cq] for r in rounded] + [r[cq:] for r in rounded], axis=1)
        y_ref[t] = jnp.dot(wo_ref[...], lat_taps(columns, lat), preferred_element_type=F32)
    for copy in edge_copies:
        copy.wait_recv()
    beside = []
    for side, rows in ((0, slice(0, ch)), (1, slice(2 * ch, 3 * ch))):
        columns = jnp.concatenate([edge_in[side, m].astype(F32)[:cq] for m in range(members)], axis=1)
        beside.append(jnp.dot(wo_ref[rows], lat_taps(columns, lat), preferred_element_type=F32))
    for m in range(members):
        def column_taps(tap, i):
            if i < 0 or i >= cols:
                return beside[0 if i < 0 else 1][:, m * lat : (m + 1) * lat]
            first = ((i // steps) * members + m) * lat
            return y_ref[i % steps, tap * ch : (tap + 1) * ch, first : first + lat]

        for i in range(cols):
            lanes = slice(i * lat, (i + 1) * lat)
            branch = column_taps(1, i) + column_taps(0, i - 1) + column_taps(2, i + 1)
            out_ref[m, :, lanes] = (f_ref[m, :, lanes].astype(F32) + branch).astype(BF16)
    for p in range(mems):
        @pl.when(z != p)
        def _(p=p):
            qk_copy(p).wait_send()
    for copy in halo_copies + list(v_copies.values()) + gm_copies + gl_copies + edge_copies:
        copy.wait_send()


def shards(mems, lons, fields, w_query, w_key, w_value, w_out):
    members, ch, cols, lat = fields.shape
    cq = w_query.shape[0]
    wide = cols * lat
    if mems != 4 or cols % 2 or cols < 4 or lat != 128 or members > 8 or (2 * cq) % 16 or ch % 16:
        return plain_shards(fields, w_query, w_key, w_value, w_out)
    score_scale = 1.0 / math.sqrt(cq * lat * cols * lons)
    dims = (mems, lons, members, ch, cq, cols, lat, score_scale)
    edge_rows = -(-cq // 16) * 16
    dma = pltpu.SemaphoreType.DMA
    vmem = pl.BlockSpec(memory_space=pltpu.VMEM)
    updated = pl.pallas_call(
        functools.partial(layer_kernel, dims),
        out_shape=jax.ShapeDtypeStruct((members, ch, wide), BF16),
        in_specs=[vmem] * 5,
        out_specs=vmem,
        scratch_shapes=[
            pltpu.VMEM((9 * cq, 3 * ch), BF16),
            pltpu.VMEM((3 * ch, 3 * cq), BF16),
            pltpu.VMEM((cols // 2, 3 * ch, 2 * members * lat), F32),
            pltpu.VMEM((2, members, ch, lat), BF16),
            pltpu.VMEM((members, cq, wide), F32),
            pltpu.VMEM((2, members, 2 * cq, lat), F32),
            pltpu.VMEM((mems * members, mems * members * cq), F32),
            pltpu.VMEM((mems, cols // 2 - 1, members, 2 * cq, lat), BF16),
            pltpu.VMEM((mems, cols // 2 - 1, members, 2 * cq, lat), BF16),
            pltpu.VMEM((cols // 2, mems, members, 2 * cq, lat), BF16),
            pltpu.VMEM((mems, 8, 128), F32),
            pltpu.VMEM((mems, 8, 128), F32),
            pltpu.VMEM((lons, 8, 128), F32),
            pltpu.VMEM((2, members, edge_rows, lat), BF16),
            pltpu.VMEM((2, members, edge_rows, lat), BF16),
            dma((2,)), dma((2,)),
            dma((mems,)), dma((mems,)),
            dma((cols // 2, mems - 1)), dma((cols // 2, mems)),
            dma((mems - 1,)), dma((mems - 1,)),
            dma((lons - 1,)), dma((lons - 1,)),
            dma((2,)), dma((2,)),
        ],
        compiler_params=pltpu.CompilerParams(
            collective_id=0, has_side_effects=True, vmem_limit_bytes=40 * 1024 * 1024
        ),
    )(fields.reshape(members, ch, wide), w_query, w_key, w_value, w_out)
    return updated.reshape(members, ch, cols, lat)


def solution(mesh):
    return jax.shard_map(
        functools.partial(shards, mesh.shape["mem"], mesh.shape["lon"]),
        mesh=mesh,
        in_specs=(P("mem", None, "lon", None), P(), P(), P(), P()),
        out_specs=P("mem", None, "lon", None),
        check_vma=False,
    )
```

```python
import functools
import math

import jax
import jax.numpy as jnp
from jax import lax
from jax.experimental import pallas as pl
from jax.experimental.pallas import tpu as pltpu
from jax.sharding import PartitionSpec as P

MESH = pl.DeviceIdType.MESH
F32 = jnp.float32
BF16 = jnp.bfloat16


def with_halo(block, sides, width):
    for axis, dim in sides:
        count = lax.axis_size(axis)
        forward = [(i, i + 1) for i in range(count - 1)]
        forward.append((count - 1, 0))
        backward = [(target, source) for source, target in forward]
        low = lax.ppermute(
            lax.slice_in_dim(block, block.shape[dim] - width, None, axis=dim), axis, forward
        )
        high = lax.ppermute(lax.slice_in_dim(block, 0, width, axis=dim), axis, backward)
        block = jnp.concatenate([low, block, high], axis=dim)
    return block


def tap_stack(extended):
    span_lon = extended.shape[2] - 2
    latitudes = extended.shape[3]
    padded = jnp.pad(extended, ((0, 0), (0, 0), (0, 0), (1, 1)))
    return jnp.concatenate(
        [
            padded[:, :, lon_step : lon_step + span_lon, lat_step : lat_step + latitudes]
            for lon_step in range(3)
            for lat_step in range(3)
        ],
        axis=1,
    )


def plain_shards(fields, w_query, w_key, w_value, w_out):
    members = fields.shape[0]
    longitudes = fields.shape[2]
    latitudes = fields.shape[3]
    inner_width = w_query.shape[0]
    extended = with_halo(fields, (("lon", 2),), 1)
    w_inner = jnp.concatenate([w_query, w_key, w_value], axis=0)
    projected = jnp.einsum(
        "oc,mcwh->mowh", w_inner, tap_stack(extended), preferred_element_type=jnp.float32
    ).astype(jnp.bfloat16)
    queries = projected[:, :inner_width]
    keys_local = projected[:, inner_width : 2 * inner_width]
    values = projected[:, 2 * inner_width :]
    query_blocks, key_blocks = (
        lax.all_to_all(queries, "mem", split_axis=3, concat_axis=0, tiled=True),
        lax.all_to_all(keys_local, "mem", split_axis=3, concat_axis=0, tiled=True),
    )
    total_members = query_blocks.shape[0]
    partial_value = jnp.dot(
        query_blocks.reshape(total_members, -1),
        key_blocks.reshape(total_members, -1).T,
        preferred_element_type=jnp.float32,
    )
    score_scale = 1.0 / math.sqrt(inner_width * latitudes * longitudes * lax.axis_size("lon"))
    first_row = lax.axis_index("mem") * members
    gram_sums = lax.psum(partial_value, ("mem", "lon"))
    weights_all = jax.nn.softmax(gram_sums * score_scale, axis=1).astype(jnp.bfloat16)
    weights_own = lax.dynamic_slice_in_dim(weights_all, first_row, members, 0)
    mixed_values = jnp.einsum(
        "mn,ncwh->mcwh",
        weights_own,
        lax.all_gather(values, "mem", axis=0, tiled=True),
        preferred_element_type=jnp.float32,
    ).astype(jnp.bfloat16)
    mixed_ext = with_halo(mixed_values, (("lon", 2),), 1)
    branch = jnp.einsum(
        "oc,mcwh->mowh", w_out, tap_stack(mixed_ext), preferred_element_type=jnp.float32
    )
    return (fields.astype(jnp.float32) + branch).astype(jnp.bfloat16)


def lat_taps(block, lat):
    width = block.shape[1]
    lane = lax.broadcasted_iota(jnp.int32, block.shape, 1) & (lat - 1)
    low = jnp.where(lane == 0, 0.0, pltpu.roll(block, 1, 1))
    high = jnp.where(lane == lat - 1, 0.0, pltpu.roll(block, width - 1, 1))
    return jnp.concatenate([low, block, high], axis=0).astype(BF16)


def shifted_sum(taps_out, rows, lat):
    zero = jnp.zeros((rows, lat), F32)
    return (
        taps_out[rows : 2 * rows]
        + jnp.concatenate([zero, taps_out[:rows, :-lat]], axis=1)
        + jnp.concatenate([taps_out[2 * rows :, lat:], zero], axis=1)
    )


def layer_kernel(
    dims, f_ref, wq_ref, wk_ref, wv_ref, w_out_ref, out_ref,
    wi_ref, wo_ref, y_ref, halo, v_raw, qk_edge, by_member, qk_out, qk_all, v_all, g_out, g_mem, g_lon, edge_out, edge_in,
    halo_s, halo_r, qk_s, qk_r, v_s, v_r, gm_s, gm_r, gl_s, gl_r, edge_s, edge_r,
):
    mems, lons, members, ch, cq, cols, lat, score_scale = dims
    wide = cols * lat
    slots = cols // 2 - 1
    is_inner = (lax.axis_index("mem") > 0) & (lax.axis_index("mem") < mems - 1)
    total = mems * members
    steps = cols // 2
    inner = 3 * cq
    z = lax.axis_index("mem")
    s = lax.axis_index("lon")
    right = lax.rem(s + 1, lons)
    left = lax.rem(s + lons - 1, lons)

    def mem_peer(d):
        return lax.rem(z + d, mems)

    def lon_peer(d):
        return lax.rem(s + d, lons)

    by_distance = [
        sorted([p for p in range(mems) if p != home], key=lambda p, home=home: (-abs(p - home), p))
        for home in range(mems)
    ]

    def far_peer(k):
        peer = by_distance[0][k]
        for home in range(1, mems):
            peer = jnp.where(z == home, by_distance[home][k], peer)
        return peer

    barrier = pltpu.get_barrier_semaphore()
    for d in range(1, mems):
        pl.semaphore_signal(barrier, inc=1, device_id={"mem": mem_peer(d)}, device_id_type=MESH)
    for d in range(1, lons):
        pl.semaphore_signal(barrier, inc=1, device_id={"lon": lon_peer(d)}, device_id_type=MESH)
    w_inner = jnp.concatenate([ref[...].astype(F32) for ref in (wq_ref, wk_ref, wv_ref)], axis=0)
    w_outer = w_out_ref[...].astype(F32)
    wi_ref[...] = jnp.concatenate([w_inner[:, a * 3 * ch : (a + 1) * 3 * ch] for a in range(3)], axis=0).astype(BF16)
    wo_ref[...] = jnp.concatenate([w_outer[:, a * 3 * cq : (a + 1) * 3 * cq] for a in range(3)], axis=0).astype(BF16)
    pl.semaphore_wait(barrier, mems + lons - 2)

    def remote(src, dst, send, recv, device):
        return pltpu.make_async_remote_copy(
            src_ref=src, dst_ref=dst, send_sem=send, recv_sem=recv, device_id=device, device_id_type=MESH
        )

    halo_copies = [
        remote(f_ref.at[:, :, pl.ds(wide - lat, lat)], halo.at[0], halo_s.at[0], halo_r.at[0], {"lon": right}),
        remote(f_ref.at[:, :, pl.ds(0, lat)], halo.at[1], halo_s.at[1], halo_r.at[1], {"lon": left}),
    ]
    for copy in halo_copies:
        copy.start()

    def qk_copy(p):
        if 0 < p < mems - 1:
            return remote(qk_out.at[p], qk_all.at[z], qk_s.at[p], qk_r.at[z], {"mem": p})
        return remote(qk_out.at[p, 0], qk_all.at[z, 0], qk_s.at[p], qk_r.at[z], {"mem": p})

    for m in range(members):
        taps = lat_taps(f_ref[m].astype(F32), lat)
        projected = shifted_sum(jnp.dot(wi_ref[...], taps, preferred_element_type=F32), inner, lat)
        queries_keys = projected[: 2 * cq]
        v_raw[m] = projected[2 * cq :]
        qk_edge[0, m] = queries_keys[:, :lat]
        qk_edge[1, m] = queries_keys[:, wide - lat :]
        for i in range(1, cols - 1):
            qk_out[1 + (i - 1) // slots, (i - 1) % slots, m] = queries_keys[:, i * lat : (i + 1) * lat].astype(BF16)
        for p in range(1, mems - 1):
            @pl.when(z != p)
            def _(p=p, m=m):
                remote(qk_out.at[p, :, m], qk_all.at[z, :, m], qk_s.at[p], qk_r.at[z], {"mem": p}).start()
    for copy in halo_copies:
        copy.wait_recv()
    beside = []
    for side, rows in ((0, slice(0, inner)), (1, slice(2 * inner, 3 * inner))):
        columns = jnp.concatenate([halo[side, m] for m in range(members)], axis=1).astype(F32)
        beside.append(jnp.dot(wi_ref[rows], lat_taps(columns, lat), preferred_element_type=F32))
    for m in range(members):
        lanes = slice(m * lat, (m + 1) * lat)
        qk_out[0, 0, m] = (qk_edge[0, m] + beside[0][: 2 * cq, lanes]).astype(BF16)
        qk_out[mems - 1, 0, m] = (qk_edge[1, m] + beside[1][: 2 * cq, lanes]).astype(BF16)
    for p in (0, mems - 1):
        @pl.when(z != p)
        def _(p=p):
            qk_copy(p).start()
    for m in range(members):
        lanes = slice(m * lat, (m + 1) * lat)
        for t in range(steps):
            upper = v_raw[m, :, t * lat : (t + 1) * lat]
            lower = v_raw[m, :, (steps + t) * lat : (steps + t + 1) * lat]
            if t == 0:
                upper = upper + beside[0][2 * cq :, lanes]
            if t == steps - 1:
                lower = lower + beside[1][2 * cq :, lanes]
            v_all[t, z, m] = jnp.concatenate([upper, lower], axis=0).astype(BF16)
    order = [0, steps - 1] + list(range(1, steps - 1))
    v_copies = {}
    for t in order:
        for k in range(mems - 1):
            v_copies[t, k] = remote(
                v_all.at[t, z], v_all.at[t, z], v_s.at[t, k], v_r.at[t, z], {"mem": far_peer(k)}
            )
    v_copies[order[0], 0].start()

    column = lax.broadcasted_iota(jnp.int32, (cq, total * cq), 1).astype(F32)
    row = lax.broadcasted_iota(jnp.int32, (cq, total * cq), 0).astype(F32)
    same = jnp.where(column - cq * jnp.floor((column + 0.5) / cq) == row, 1.0, 0.0)
    spread = lax.broadcasted_iota(jnp.int32, (total * cq, 128), 0) - cq * lax.broadcasted_iota(
        jnp.int32, (total * cq, 128), 1
    )
    groups = jnp.where((spread >= 0) & (spread < cq), 1.0, 0.0)
    def add_columns(first, count):
        parts = [qk_all[:, first + j].astype(F32).reshape(total, 2 * cq, lat) for j in range(count)]
        both = jnp.concatenate(parts, axis=2)
        queries = both[:, :cq].reshape(total * cq, count * lat).astype(BF16)
        keys = both[:, cq:].reshape(total * cq, count * lat).astype(BF16)
        products = lax.dot_general(queries, keys, (((1,), (1,)), ((), ())), preferred_element_type=F32)
        return jnp.sum(products.reshape(total, cq, total * cq) * same[None], axis=1)

    @pl.when(is_inner)
    def _():
        qk_all[z] = qk_out[z]
        for d in range(1, mems):
            source = mem_peer(d)
            remote(qk_out.at[source], qk_all.at[source], qk_s.at[0], qk_r.at[source], {"mem": source}).wait_recv()
        by_member[...] = add_columns(0, slots)

    @pl.when(jnp.logical_not(is_inner))
    def _():
        qk_all[z, 0] = qk_out[z, 0]
        for d in range(1, mems):
            source = mem_peer(d)
            remote(
                qk_out.at[source, 0], qk_all.at[source, 0], qk_s.at[0], qk_r.at[source], {"mem": source}
            ).wait_recv()
        by_member[...] = add_columns(0, 1)

    gram = jnp.dot(by_member[...], groups, precision=lax.Precision.HIGHEST, preferred_element_type=F32)
    filler = jnp.zeros((8 - members, 128), F32)
    for p in range(mems):
        g_out[p] = jnp.concatenate([gram[p * members : (p + 1) * members], filler], axis=0)
    gm_copies = [
        remote(g_out.at[mem_peer(d)], g_mem.at[z], gm_s.at[d - 1], gm_r.at[d - 1], {"mem": mem_peer(d)})
        for d in range(1, mems)
    ]
    for copy in gm_copies:
        copy.start()
    for t in order:
        for k in range(1 if t == order[0] else 0, mems - 1):
            v_copies[t, k].start()
    g_mem[z] = g_out[z]
    for copy in gm_copies:
        copy.wait_recv()
    g_lon[s] = jnp.sum(g_mem[...], axis=0)
    gl_copies = [
        remote(g_lon.at[s], g_lon.at[s], gl_s.at[d - 1], gl_r.at[d - 1], {"lon": lon_peer(d)})
        for d in range(1, lons)
    ]
    for copy in gl_copies:
        copy.start()
    for copy in gl_copies:
        copy.wait_recv()
    lane = lax.broadcasted_iota(jnp.int32, (8, 128), 1)
    scores = jnp.where(lane < total, jnp.sum(g_lon[...], axis=0) * score_scale, -jnp.inf)
    powers = jnp.exp(scores - jnp.max(scores, axis=1, keepdims=True))
    weights = (powers / jnp.sum(powers, axis=1, keepdims=True)).astype(BF16).astype(F32)

    edge_copies = [
        remote(edge_out.at[0], edge_in.at[0], edge_s.at[0], edge_r.at[0], {"lon": right}),
        remote(edge_out.at[1], edge_in.at[1], edge_s.at[1], edge_r.at[1], {"lon": left}),
    ]
    edge_pad = jnp.zeros((edge_out.shape[2] - cq, lat), F32)
    for t in order:
        for d in range(1, mems):
            source = mem_peer(d)
            remote(v_all.at[t, source], v_all.at[t, source], v_s.at[t, 0], v_r.at[t, source], {"mem": source}).wait_recv()
        sums = [None] * members
        for n in range(total):
            block = v_all[t, n // members, n % members].astype(F32)
            for m in range(members):
                term = weights[m : m + 1, n : n + 1] * block
                sums[m] = term if n == 0 else sums[m] + term
        rounded = [sums[m].astype(BF16).astype(F32) for m in range(members)]
        if t == 0:
            for m in range(members):
                edge_out[1, m] = jnp.concatenate([rounded[m][:cq], edge_pad], axis=0).astype(BF16)
            edge_copies[1].start()
        if t == steps - 1:
            for m in range(members):
                edge_out[0, m] = jnp.concatenate([rounded[m][cq:], edge_pad], axis=0).astype(BF16)
            edge_copies[0].start()
        columns = jnp.concatenate([r[:cq] for r in rounded] + [r[cq:] for r in rounded], axis=1)
        y_ref[t] = jnp.dot(wo_ref[...], lat_taps(columns, lat), preferred_element_type=F32)
    for copy in edge_copies:
        copy.wait_recv()
    beside = []
    for side, rows in ((0, slice(0, ch)), (1, slice(2 * ch, 3 * ch))):
        columns = jnp.concatenate([edge_in[side, m].astype(F32)[:cq] for m in range(members)], axis=1)
        beside.append(jnp.dot(wo_ref[rows], lat_taps(columns, lat), preferred_element_type=F32))
    for m in range(members):
        def column_taps(tap, i):
            if i < 0 or i >= cols:
                return beside[0 if i < 0 else 1][:, m * lat : (m + 1) * lat]
            first = ((i // steps) * members + m) * lat
            return y_ref[i % steps, tap * ch : (tap + 1) * ch, first : first + lat]

        for i in range(cols):
            lanes = slice(i * lat, (i + 1) * lat)
            branch = column_taps(1, i) + column_taps(0, i - 1) + column_taps(2, i + 1)
            out_ref[m, :, lanes] = (f_ref[m, :, lanes].astype(F32) + branch).astype(BF16)
    for p in range(mems):
        @pl.when(z != p)
        def _(p=p):
            qk_copy(p).wait_send()
    for copy in halo_copies + list(v_copies.values()) + gm_copies + gl_copies + edge_copies:
        copy.wait_send()


def shards(mems, lons, fields, w_query, w_key, w_value, w_out):
    members, ch, cols, lat = fields.shape
    cq = w_query.shape[0]
    wide = cols * lat
    if mems != 4 or cols % 2 or cols < 4 or lat != 128 or members > 8 or (2 * cq) % 16 or ch % 16:
        return plain_shards(fields, w_query, w_key, w_value, w_out)
    score_scale = 1.0 / math.sqrt(cq * lat * cols * lons)
    dims = (mems, lons, members, ch, cq, cols, lat, score_scale)
    edge_rows = -(-cq // 16) * 16
    dma = pltpu.SemaphoreType.DMA
    vmem = pl.BlockSpec(memory_space=pltpu.VMEM)
    updated = pl.pallas_call(
        functools.partial(layer_kernel, dims),
        out_shape=jax.ShapeDtypeStruct((members, ch, wide), BF16),
        in_specs=[vmem] * 5,
        out_specs=vmem,
        scratch_shapes=[
            pltpu.VMEM((9 * cq, 3 * ch), BF16),
            pltpu.VMEM((3 * ch, 3 * cq), BF16),
            pltpu.VMEM((cols // 2, 3 * ch, 2 * members * lat), F32),
            pltpu.VMEM((2, members, ch, lat), BF16),
            pltpu.VMEM((members, cq, wide), F32),
            pltpu.VMEM((2, members, 2 * cq, lat), F32),
            pltpu.VMEM((mems * members, mems * members * cq), F32),
            pltpu.VMEM((mems, cols // 2 - 1, members, 2 * cq, lat), BF16),
            pltpu.VMEM((mems, cols // 2 - 1, members, 2 * cq, lat), BF16),
            pltpu.VMEM((cols // 2, mems, members, 2 * cq, lat), BF16),
            pltpu.VMEM((mems, 8, 128), F32),
            pltpu.VMEM((mems, 8, 128), F32),
            pltpu.VMEM((lons, 8, 128), F32),
            pltpu.VMEM((2, members, edge_rows, lat), BF16),
            pltpu.VMEM((2, members, edge_rows, lat), BF16),
            dma((2,)), dma((2,)),
            dma((mems,)), dma((mems,)),
            dma((cols // 2, mems - 1)), dma((cols // 2, mems)),
            dma((mems - 1,)), dma((mems - 1,)),
            dma((lons - 1,)), dma((lons - 1,)),
            dma((2,)), dma((2,)),
        ],
        compiler_params=pltpu.CompilerParams(
            collective_id=0, has_side_effects=True, vmem_limit_bytes=40 * 1024 * 1024
        ),
    )(fields.reshape(members, ch, wide), w_query, w_key, w_value, w_out)
    return updated.reshape(members, ch, cols, lat)


def solution(mesh):
    return jax.shard_map(
        functools.partial(shards, mesh.shape["mem"], mesh.shape["lon"]),
        mesh=mesh,
        in_specs=(P("mem", None, "lon", None), P(), P(), P(), P()),
        out_specs=P("mem", None, "lon", None),
        check_vma=False,
    )
```
